32 devices in a mesh: groups: 2 (over x), dev: 8 (over z, y), sub: 2 (over core).
Axes of the slice: x: 2, y: 2, z: 4, core: 2. Of those that a mesh axis runs over, the one named last changes fastest.
Arguments:
- hidden: bfloat16 [1024, 2048], P(('groups', 'dev', 'sub')), parts along dimension 0, may hold values from -6 to 6
- lengths: int32 [32, 32], P(('groups', 'dev', 'sub')), parts along dimension 0, may hold values from 1 to 256, 4096 in all within a row
- key_cache: bfloat16 [32, 4096, 512], P(('groups', 'dev', 'sub')), parts along dimension 0, may hold values from -320 to 320
- value_cache: bfloat16 [32, 4096, 512], P(('groups', 'dev', 'sub')), parts along dimension 0, may hold values from -6 to 6
- expert_ids: int32 [1024, 8], P(('groups', 'dev', 'sub')), parts along dimension 0, may hold values from 0 to 15, all different within a row; in each aligned block of 32 rows (0 to 31, 32 to 63, ...) at most 16 rows name the same one
- gate_codes: int32 [1024, 8], P(('groups', 'dev', 'sub')), parts along dimension 0, may hold values from 1 to 1023
- expert_device: int32 [16], replicated, may hold values from 0 to 15, each once
- attention_gain: float32 [2048], replicated, may hold values from 0.1 to 1.9
- mixture_gain: float32 [2048], replicated, may hold values from 0.1 to 1.9
- query_gain: float32 [128], replicated, may hold values from 0.1 to 1.9
- key_gain: float32 [128], replicated, may hold values from 0.1 to 1.9
- project_weight: bfloat16 [2048, 5120], P(None, 'dev'), may hold values from -0.125 to 0.125
- output_weight: bfloat16 [4096, 2048], P('dev'), may hold values from -0.09375 to 0.09375
- expert_gate_up: bfloat16 [16, 2048, 1536], P(('dev', 'sub')), may hold values from -0.125 to 0.125
- expert_down: bfloat16 [16, 768, 2048], P(('dev', 'sub')), may hold values from -0.21875 to 0.21875
Outputs:
- layer_out: bfloat16 [1024, 2048], P(('groups', 'dev', 'sub')), parts along dimension 0
The draws below stay inside these ranges and needn't reach their ends.
There are 2 independent parts, one for each index of `groups`. The reference program is written for one: setup_inputs(seed, part) draws one part's arguments, and reference() takes and returns one part's arrays. A program takes and returns all parts, laid end to end along the dimension named above; an argument that names none is the same for every part. Nothing has to cross between parts.
Inputs may be any that keep to these rules, and one draw needn't show every extreme that they name: `expert_ids`: each row names 8 different experts. Among the 32 rows of one device no expert is named more than 16 times, and in some device an expert is named exactly 16 times. The 32 lengths of each device sum to 4096; the largest of them is 256. A permutation: expert e is held by the device at index expert_device[e] of the joined axes dev and sub.
All inputs are finite; a program needn't handle non-finite values.
Results may differ from the reference program's by a relative error of at most 0.015.
Values may be sent and summed in bfloat16 or wider, within the bound.
No kernel may reach another device: no remote copies, remote signals or barrier semaphores. Data moves between devices by JAX's collectives and lax.ppermute only.
A program may use at most 128 MiB of HBM per device.

```python
import math
import jax
import jax.numpy as jnp
import numpy as np
from jax import lax

D = 2048
HEADS = 32
KVH = 4
HD = 128
FF = 768
TOP = 8
R_DEV = 32
POOL = 4096
LMOST = 256
CAP = 16
GROUP_DEVS = 16
EXPERTS = 16
ROWS = 512
QKV = 5120


def draw_key_cache(key, part):
    normal_key = jax.random.fold_in(jax.random.fold_in(key, 7), 0)
    array_shape = (GROUP_DEVS, POOL, KVH * HD)
    normal_part = jnp.clip(jax.random.normal(normal_key, array_shape, jnp.float32), -8.0, 8.0)
    return normal_part.astype(jnp.bfloat16)


def with_ends(entries, key, smallest, high):
    place = [jax.random.randint(jax.random.fold_in(key, axis), (), 0, length) for axis, length in enumerate(entries.shape)]
    longest = entries.shape.index(max(entries.shape))
    beside = place[:longest] + [(place[longest] + 1) % entries.shape[longest]] + place[longest + 1:]
    return entries.at[tuple(place)].set(smallest).at[tuple(beside)].set(high)


def block_levels(key, dims, shards, least, largest):
    def one(axis_at, blocks):
        heights = jax.random.uniform(jax.random.fold_in(jax.random.fold_in(key, 6), axis_at), (blocks,), jnp.float32, least / len(shards), largest / len(shards))
        return jnp.repeat(jnp.exp(heights), dims[axis_at] // blocks).reshape((-1,) + (1,) * (len(dims) - axis_at - 1))

    factor_of = one(*shards[0])
    for cut in shards[1:]:
        factor_of = factor_of * one(*cut)
    return factor_of


def profile(count, total, bound, lean):
    portions = [(1 << 20) // math.isqrt(grade ** lean) + 1 for grade in range(2, count + 1)]
    spare, holding = total - bound - (count - 1), [1] * (count - 1)
    while spare > 0:
        free = [i for i in range(count - 1) if holding[i] < bound]
        whole, budget = sum([portions[i] for i in free]), spare
        for i in free:
            more = min(bound - holding[i], max(1, budget * portions[i] // whole), spare)
            holding[i] = holding[i] + more
            spare = spare - more
    return np.array([bound] + holding)


def uneven(stream_key, number_of, total, bound, lean):
    if number_of == 2:
        one = jax.random.randint(stream_key, (), max(1, total - bound), min(bound, total - 1) + 1)
        return jnp.stack([one, total - one])
    sizes = jnp.asarray(profile(number_of, total, bound, lean), jnp.int32)
    couples = (number_of - 1) // 2
    donor, receiver = sizes[1:1 + 2 * couples:2], sizes[2:2 + 2 * couples:2]
    room = jnp.minimum(donor - 1, bound - receiver)
    shifted = jax.random.randint(jax.random.fold_in(stream_key, 1), (couples,), 0, 1 << 20) % (room + 1)
    sizes = sizes.at[1:1 + 2 * couples:2].set(donor - shifted).at[2:2 + 2 * couples:2].set(receiver + shifted)
    return sizes[jax.random.permutation(jax.random.fold_in(stream_key, 2), number_of)]


def shared_out(key, own, number, rows, number_of, top, reach, slope):
    order = jax.random.permutation(key, number_of)
    heavy_load, common = shares(number_of, rows * top, reach, slope, True), shares(number_of, rows * top, reach, slope, False)
    places = jnp.arange(number_of)

    def named(sizes, turn):
        used = int((sizes > 0).sum())
        fixed = max(1, used // 4)
        moved = fixed + (places - fixed + turn * (used - fixed)) % max(1, number_of - fixed)
        return jnp.zeros((number_of,), jnp.int32).at[order[jnp.where(places < fixed, places, moved)]].set(jnp.asarray(sizes, jnp.int32))

    sizes = jnp.where(number % 4 == 0, named(heavy_load, number // 4), named(common, number - number // 4 - 1))
    mixed = jax.random.permutation(jax.random.fold_in(own, 3), number_of)
    giver, taker = mixed[0:number_of // 2 * 2:2], mixed[1:number_of // 2 * 2:2]
    room = jnp.minimum(sizes[giver] - 1, reach - sizes[taker]) // 2
    room = jnp.where((giver == order[0]) | (taker == order[0]) | (sizes[taker] == 0), 0, jnp.maximum(room, 0))
    moved = jax.random.randint(jax.random.fold_in(own, 4), (number_of // 2,), 0, 1 << 20) % (room + 1)
    sizes = sizes.at[giver].add(-moved).at[taker].add(moved)
    items = jnp.searchsorted(jnp.cumsum(sizes), jnp.arange(rows * top), side="right").astype(jnp.int32)
    grid = items.reshape(top, rows).T
    grid = grid[jax.random.permutation(jax.random.fold_in(own, 1), rows)]
    turn = jax.random.randint(jax.random.fold_in(own, 2), (rows, 1), 0, top)
    return jnp.take_along_axis(grid, (jnp.arange(top)[None, :] + turn) % top, axis=1)


def shares(count, total, most, slope, full):
    weights = [(1 << 20) // math.isqrt(grade ** slope) + 1 for grade in range(1, count + 1)]
    largest = most if full else min(most, max(-(-total // count), total * weights[0] // sum(weights)))
    least = 1 if total - largest >= count - 1 else 0
    holding, spare = [largest] + [least] * (count - 1), total - largest - least * (count - 1)
    while spare > 0:
        free = [i for i in range(1, count) if holding[i] < largest] or [i for i in range(1, count) if holding[i] < most]
        whole, budget = sum([weights[i] for i in free]), spare
        for i in free:
            more = min(most - holding[i], max(1, budget * weights[i] // whole), spare)
            holding[i] = holding[i] + more
            spare = spare - more
    return np.array(holding)


def centred(key, shape, deviation, most, cuts=(), held_as=jnp.bfloat16):
    factor_of = block_levels(key, shape, cuts, -0.22, 0.18) if cuts else 1.0
    array = jax.random.normal(key, shape, jnp.float32) * deviation * factor_of
    return jnp.minimum(jnp.maximum(array, -most), most).astype(held_as)


def setup_inputs(seed: int = 0, part: int = 0) -> dict:
    streams_of = jax.random.split(jax.random.key(seed), 16)
    part_splits = jax.random.split(jax.random.fold_in(streams_of[15], part), 16)
    hidden = centred(part_splits[0], (ROWS, D), 1.0, 6.0, ((0, 16),))
    lengths = jax.vmap(lambda own: uneven(own, R_DEV, POOL, LMOST, 2))(jax.random.split(part_splits[1], GROUP_DEVS)).reshape((GROUP_DEVS, R_DEV)).astype(jnp.int32)
    key_cache = draw_key_cache(jax.random.fold_in(jax.random.fold_in(streams_of[15], part), 71), part)
    value_cache = centred(part_splits[3], (GROUP_DEVS, POOL, KVH * HD), 1.0, 6.0, ((0, 16),))
    expert_ids_keys = jax.random.split(jax.random.fold_in(part_splits[4], 1), ROWS // R_DEV)
    expert_ids_turns = jax.random.permutation(jax.random.fold_in(part_splits[4], 3), ROWS // R_DEV)
    expert_ids = jax.vmap(lambda own, number: shared_out(jax.random.fold_in(part_splits[4], 2), own, number, R_DEV, EXPERTS, TOP, CAP, 2))(expert_ids_keys, expert_ids_turns).reshape((ROWS, TOP))
    gate_codes = with_ends(jax.random.randint(part_splits[5], (ROWS, TOP), 1, 1024), jax.random.fold_in(part_splits[5], 1), 1, 1023).astype(jnp.int32)
    expert_device = jax.random.permutation(streams_of[6], EXPERTS).astype(jnp.int32)
    attention_gain = jnp.clip(1.0 + 0.18 * jax.random.normal(streams_of[7], (D,), jnp.float32), 0.1, 1.9)
    mixture_gain = jnp.clip(1.0 + 0.18 * jax.random.normal(streams_of[8], (D,), jnp.float32), 0.1, 1.9)
    query_gain = jnp.clip(1.0 + 0.18 * jax.random.normal(streams_of[9], (HD,), jnp.float32), 0.1, 1.9)
    key_gain = jnp.clip(1.0 + 0.18 * jax.random.normal(streams_of[10], (HD,), jnp.float32), 0.1, 1.9)
    project_weight = centred(streams_of[11], (D, QKV), D ** -0.5, 0.125, ((1, 8),))
    output_weight = centred(streams_of[12], (HEADS * HD, D), (HEADS * HD) ** -0.5, 0.09375, ((0, 8),))
    expert_gate_up = centred(streams_of[13], (EXPERTS, D, 2 * FF), D ** -0.5, 0.125, ((0, 16),))
    expert_down = centred(streams_of[14], (EXPERTS, FF, D), FF ** -0.5, 0.21875, ((0, 16),))
    return {"hidden": hidden, "lengths": lengths, "key_cache": key_cache, "value_cache": value_cache, "expert_ids": expert_ids, "gate_codes": gate_codes, "expert_device": expert_device, "attention_gain": attention_gain, "mixture_gain": mixture_gain, "query_gain": query_gain, "key_gain": key_gain, "project_weight": project_weight, "output_weight": output_weight, "expert_gate_up": expert_gate_up, "expert_down": expert_down}


EPSILON = 1e-06
ROPE_BASE = 1000000.0

def norm_scale(values, scale_gain):
    mean_square = lax.optimization_barrier(jnp.mean(values * values, axis=-1, keepdims=True))
    return values * lax.rsqrt(mean_square + EPSILON) * scale_gain

def rotate(values, position):
    half_width = values.shape[-1] // 2
    frequency = ROPE_BASE ** (-jnp.arange(half_width, dtype=jnp.float32) * 2.0 / values.shape[-1])
    angles = position.astype(jnp.float32)[:, None] * frequency[None, :]
    cosine = jnp.cos(angles)[:, None, :]
    sine_part = jnp.sin(angles)[:, None, :]
    first_half = values[..., :half_width]
    second_half = values[..., half_width:]
    return jnp.concatenate([first_half * cosine - second_half * sine_part, second_half * cosine + first_half * sine_part], axis=-1)

def split_heads(merged, position, query_gain, key_gain):
    row_count = merged.shape[0]
    query_cols = HEADS * HD
    key_cols = KVH * HD
    queries = merged[:, :query_cols].astype(jnp.float32).reshape(row_count, HEADS, HD)
    queries = rotate(norm_scale(queries, query_gain), position).astype(jnp.bfloat16)
    new_keys = merged[:, query_cols:query_cols + key_cols].astype(jnp.float32).reshape(row_count, KVH, HD)
    new_keys = rotate(norm_scale(new_keys, key_gain), position).astype(jnp.bfloat16)
    new_values = merged[:, query_cols + key_cols:].reshape(row_count, KVH, HD)
    return (queries, new_keys, new_values)

def attend(queries, new_keys, new_values, key_rows, value_rows, lengths):
    row_count, head_count, head_width = queries.shape
    kv_count = new_keys.shape[1]
    group_size = head_count // kv_count
    pool_size = key_rows.shape[0]
    seg_end = jnp.cumsum(lengths).astype(jnp.int32)
    seg_start = seg_end - lengths
    position = jnp.arange(pool_size, dtype=jnp.int32)
    inside = (position[None, :] >= seg_start[:, None]) & (position[None, :] < seg_end[:, None])
    grouped = queries.reshape(row_count, kv_count, group_size, head_width).astype(jnp.float32)
    keyed = key_rows.reshape(pool_size, kv_count, head_width).astype(jnp.float32)
    valued = value_rows.reshape(pool_size, kv_count, head_width).astype(jnp.float32)
    scale = 1.0 / math.sqrt(head_width)
    scores = jnp.einsum('rkgd,pkd->krgp', grouped, keyed) * scale
    own_score = jnp.einsum('rkgd,rkd->krg', grouped, new_keys.astype(jnp.float32)) * scale
    mask = inside[None, :, None, :]
    masked = jnp.where(mask, scores, -1e+30)
    peak = jnp.maximum(lax.optimization_barrier(jnp.max(masked, axis=3)), own_score)
    raised = jnp.where(mask, jnp.exp(masked - peak[..., None]), 0.0)
    own_raised = jnp.exp(own_score - peak)
    denominator = lax.optimization_barrier(jnp.sum(raised, axis=3)) + own_raised
    weights = (raised / denominator[..., None]).astype(jnp.bfloat16)
    mixed_out = jnp.einsum('krgp,pkd->rkgd', weights.astype(jnp.float32), valued)
    own_weight = jnp.transpose(own_raised / denominator, (1, 0, 2))[..., None]
    own_part = own_weight * new_values.astype(jnp.float32)[:, :, None, :]
    return (mixed_out + own_part).reshape(row_count, head_count * head_width).astype(jnp.bfloat16)

def reference(hidden, lengths, key_cache, value_cache, expert_ids, gate_codes, expert_device, attention_gain, mixture_gain, query_gain, key_gain, project_weight, output_weight, expert_gate_up, expert_down):
    row_count = hidden.shape[0]
    normed = norm_scale(hidden.astype(jnp.float32), attention_gain).astype(jnp.bfloat16)
    merged = jnp.dot(normed, project_weight, preferred_element_type=jnp.float32).astype(jnp.bfloat16)
    position = lengths.reshape(row_count)
    queries, new_keys, new_values = split_heads(merged, position, query_gain, key_gain)

    def per_block(blocks):
        return attend(blocks[0], blocks[1], blocks[2], blocks[3], blocks[4], blocks[5])
    attention = lax.map(per_block, (queries.reshape(GROUP_DEVS, R_DEV, HEADS, HD), new_keys.reshape(GROUP_DEVS, R_DEV, KVH, HD), new_values.reshape(GROUP_DEVS, R_DEV, KVH, HD), key_cache, value_cache, lengths))
    attention = attention.reshape(row_count, HEADS * HD)
    residual = hidden.astype(jnp.float32) + jnp.dot(attention, output_weight, preferred_element_type=jnp.float32)
    mixture_in = norm_scale(residual, mixture_gain).astype(jnp.bfloat16)
    share = gate_codes.astype(jnp.float32)
    share = share / lax.optimization_barrier(jnp.sum(share, axis=1, keepdims=True))
    holder = jnp.take(expert_device, expert_ids).astype(jnp.int32)
    row_limit = min(row_count, CAP * GROUP_DEVS)

    def one_slot(total, slot_index):
        hits = holder == slot_index
        weight = lax.optimization_barrier(jnp.sum(jnp.where(hits, share, 0.0), axis=1))
        chosen = jnp.any(hits, axis=1).astype(jnp.int32)
        ranking = jnp.argsort(1 - chosen, stable=True)[:row_limit].astype(jnp.int32)
        picked = jnp.take(mixture_in, ranking, axis=0)
        both_parts = jnp.dot(picked, expert_gate_up[slot_index], preferred_element_type=jnp.float32)
        units = (jax.nn.silu(both_parts[:, :FF]) * both_parts[:, FF:]).astype(jnp.bfloat16)
        expert_out = jnp.dot(units, expert_down[slot_index], preferred_element_type=jnp.float32).astype(jnp.bfloat16)
        addition = expert_out.astype(jnp.float32) * jnp.take(weight, ranking)[:, None]
        return (total.at[ranking].add(addition), None)
    routed, unused = lax.scan(one_slot, jnp.zeros((row_count, D), jnp.float32), jnp.arange(GROUP_DEVS, dtype=jnp.int32))
    return (residual + routed).astype(jnp.bfloat16)
```

```python
import functools
import math

import jax
import jax.numpy as jnp
from jax import lax
from jax.experimental import pallas as pl
from jax.experimental.pallas import tpu as pltpu
from jax.sharding import PartitionSpec as P

HD = 128

EPSILON = 1e-06
ROPE_BASE = 1000000.0
LOG2E = 1.4426950408889634
LONGEST = 256
ALIGN = 16
WINDOW = LONGEST + ALIGN
UNROLL = 8
TILE = 256


def norm_scale(values, scale_gain):
    mean_square = jnp.mean(values * values, axis=-1, keepdims=True)
    return values * lax.rsqrt(mean_square + EPSILON) * scale_gain


def ring_order(count):
    return list(range(0, count, 2)) + list(range(1, count, 2))[::-1]


class Ring:
    def __init__(self, count):
        self.count = count
        self.far = count // 2
        order = ring_order(count)
        self.forward = [(order[i], order[(i + 1) % count]) for i in range(count)]
        self.backward = [(b, a) for a, b in self.forward]
        self.distances = [0]
        for step in range(1, self.far):
            self.distances += [step, -step]
        self.distances += [self.far]

    def ahead(self, values):
        return lax.ppermute(values, "dev", self.forward)

    def behind(self, values):
        return lax.ppermute(values, "dev", self.backward)

    def owners(self):
        count = self.count
        device = lax.axis_index("dev").astype(jnp.int32)
        index = lax.broadcasted_iota(jnp.int32, (1, count), 1)
        step = (index + 1) // 2
        distance = jnp.where(index % 2 == 1, step, -step)
        place = jnp.where(device % 2 == 0, device // 2, count - 1 - device // 2)
        place = place + distance
        place = jnp.where(place < 0, place + count, place)
        place = jnp.where(place >= count, place - count, place)
        return jnp.where(place < self.far, 2 * place, 2 * (count - 1 - place) + 1)


def ring_gather(ring, block):
    half_rows = block.shape[0] // 2
    up, down = block, block
    pieces = [block]
    for step in range(1, ring.far):
        up, down = ring.ahead(up), ring.behind(down)
        pieces += [down, up]
    pieces += [ring.ahead(up[:half_rows]), ring.behind(down[half_rows:])]
    return jnp.concatenate(pieces, axis=0), pieces


def ring_scatter_sum(ring, far_up, far_down, ups, downs):
    half_width = far_up.shape[1]
    sent = jnp.bfloat16
    up, down = ring.ahead(far_up), ring.behind(far_down)
    for distance in range(ring.far - 1, 0, -1):
        mine_up, mine_down = ups[distance - 1], downs[distance - 1]
        up, down = up.astype(jnp.float32), down.astype(jnp.float32)
        if distance == ring.far - 1:
            up = jnp.concatenate([mine_up[:, :half_width] + up, mine_up[:, half_width:]], axis=1)
            down = jnp.concatenate(
                [mine_down[:, :half_width], mine_down[:, half_width:] + down], axis=1
            )
        else:
            up, down = mine_up + up, mine_down + down
        up, down = ring.ahead(up.astype(sent)), ring.behind(down.astype(sent))
    return up, down


def whole_blocks(kinds):
    return [pl.BlockSpec(memory_space=kind) for kind in kinds]


def call(body, outs, ins, operands, scratch, limit, name, cost=100):
    return pl.pallas_call(
        body,
        out_shape=outs,
        in_specs=whole_blocks(ins),
        out_specs=jax.tree.map(lambda _: pl.BlockSpec(memory_space=pltpu.VMEM), outs),
        scratch_shapes=scratch,
        cost_estimate=pl.CostEstimate(
            flops=0, bytes_accessed=cost * 1024 * 1024, transcendentals=0
        ),
        compiler_params=pltpu.CompilerParams(vmem_limit_bytes=limit * 1024 * 1024),
        name=name,
    )(*operands)


VMEM, SMEM, HBM, ANY = pltpu.VMEM, pltpu.SMEM, pltpu.HBM, pl.ANY


def start_copies(pairs, sems):
    copies = [
        pltpu.make_async_copy(source, target, sems.at[index])
        for index, (source, target) in enumerate(pairs)
    ]
    for copy in copies:
        copy.start()
    return copies


def norm_kernel(hidden_hbm, gain_hbm, out_ref, hidden_ref, gain_ref, sems):
    pairs = [(hidden_hbm, hidden_ref), (gain_hbm, gain_ref)]
    for copy in start_copies(pairs, sems):
        copy.wait()
    values = hidden_ref[...].astype(jnp.float32)
    out_ref[...] = norm_scale(values, gain_ref[...]).astype(jnp.bfloat16)


def digit_kernel(holder_ref, ids_ref, codes_ref, out_ref):
    ids, codes = ids_ref[...], codes_ref[...]
    lane = lax.broadcasted_iota(jnp.int32, out_ref.shape, 1)
    high = jnp.zeros(out_ref.shape, jnp.float32)
    for expert in range(holder_ref.shape[1]):
        code = jnp.sum(jnp.where(ids == expert, codes, 0), axis=1, keepdims=True)
        slot = holder_ref[0, expert]
        high = high + jnp.where(lane == slot, (code >> 5).astype(jnp.float32), 0.0)
        high = high + jnp.where(lane == slot + HD // 2, (code & 31).astype(jnp.float32), 0.0)
    out_ref[...] = high.astype(jnp.bfloat16)


def load_kernel(number, *refs):
    sources, targets, sems = refs[:number], refs[-1 - number : -1], refs[-1]
    for copy in start_copies(list(zip(sources, targets)), sems):
        copy.wait()


def loaded(arrays, after, limit, name):
    number = len(arrays)
    return call(
        functools.partial(load_kernel, number),
        [jax.ShapeDtypeStruct(array.shape, array.dtype) for array in arrays],
        [HBM] * number + [ANY],
        (*arrays, after),
        [pltpu.SemaphoreType.DMA((number,))],
        limit,
        name,
    )


def project_kernel(count, owner_ref, normed_ref, weight_ref, out_ref):
    rows = normed_ref.shape[0] // count
    product = jnp.dot(normed_ref[...], weight_ref[...], preferred_element_type=jnp.float32)
    product = product.astype(jnp.bfloat16)
    for index in range(count):
        out_ref[owner_ref[0, index]] = product[index * rows : (index + 1) * rows]


def output_kernel(count, owner_ref, feature_ref, weight_ref, *refs):
    outs, held = refs[:-1], refs[-1]
    rows = feature_ref.shape[1]
    for index in range(count):
        held[index * rows : (index + 1) * rows, :] = feature_ref[owner_ref[0, index]]
    product = jnp.dot(held[...], weight_ref[...], preferred_element_type=jnp.float32)
    split_blocks(count, rows, product, outs)


def split_blocks(count, rows, product, outs):
    own, far_up, far_down, ups, downs = outs
    half_width = product.shape[1] // 2
    own[...] = product[:rows]
    for index in range(1, count - 1):
        side = ups if index % 2 else downs
        side[(index - 1) // 2] = product[index * rows : (index + 1) * rows]
    last = product[(count - 1) * rows :].astype(jnp.bfloat16)
    far_up[...] = last[:, :half_width]
    far_down[...] = last[:, half_width:]


def block_shapes(count, rows, width):
    own = jax.ShapeDtypeStruct((rows, width), jnp.float32)
    half = jax.ShapeDtypeStruct((rows, width // 2), jnp.bfloat16)
    side = jax.ShapeDtypeStruct((count // 2 - 1, rows, width), jnp.float32)
    return [own, half, half, side, side]


def residual_kernel(
    hidden_ref, own_ref, up_ref, down_ref, gain_ref, digit_ref, residual_ref, sent_ref
):
    width = hidden_ref.shape[1]
    summed = own_ref[...] + up_ref[...].astype(jnp.float32) + down_ref[...].astype(jnp.float32)
    residual = hidden_ref[...].astype(jnp.float32) + summed
    residual_ref[...] = residual
    sent_ref[:, :width] = norm_scale(residual, gain_ref[...]).astype(jnp.bfloat16)
    sent_ref[:, width:] = digit_ref[...]


def expert_kernel(count, slots, slot_ref, held, *refs):
    subs = slot_ref.shape[1]
    gate_ups, downs, refs = refs[:subs], refs[subs : 2 * subs], refs[2 * subs :]
    outs, (units, total) = refs[:5], refs[5:]
    width = total.shape[1]
    inner = units.shape[1]
    rows = held.shape[0] // count
    digits = held[:, width:].astype(jnp.float32)
    lane = lax.broadcasted_iota(jnp.int32, digits.shape, 1)
    codes = digits * 32.0 + pltpu.roll(digits, HD // 2, 1)
    codes = jnp.where(lane < slots, codes, 0.0)
    whole = jnp.sum(codes, axis=1, keepdims=True)
    for shift in range(subs):
        mine = jnp.where(lane == slot_ref[0, shift], codes, 0.0)
        weight = jnp.sum(mine, axis=1, keepdims=True) / whole
        for start in range(0, inner, TILE):
            gate, up = [
                jnp.dot(
                    held[:, :width],
                    gate_ups[shift][:, column : column + TILE],
                    preferred_element_type=jnp.float32,
                )
                for column in (start, inner + start)
            ]
            units[:, start : start + TILE] = (jax.nn.silu(gate) * up).astype(jnp.bfloat16)
        for start in range(0, width, 2 * TILE):
            columns = slice(start, start + 2 * TILE)
            result = jnp.dot(
                units[...], downs[shift][:, columns], preferred_element_type=jnp.float32
            )
            result = result.astype(jnp.bfloat16).astype(jnp.float32) * weight
            if shift:
                result = result + total[:, columns]
            total[:, columns] = result
    split_blocks(count, rows, total, outs)


def attention_kernel(
    kv_count,
    length_ref,
    merged_ref,
    cos_ref,
    sin_ref,
    query_gain_ref,
    key_gain_ref,
    key_ref,
    value_ref,
    *refs,
):
    out_ref, queries, results, new_keys, new_values, start_ref = refs[-6:]
    rows = merged_ref.shape[1]
    heads = queries.shape[0] // rows
    group = heads // kv_count
    pool = key_ref.shape[0]
    per_block = merged_ref.shape[2] // HD
    scale = LOG2E / math.sqrt(HD)

    def head(index):
        block, slot = index // per_block, index % per_block
        return merged_ref[block, :, slot * HD : (slot + 1) * HD].astype(jnp.float32)

    def turned(values, gain):
        mean_square = jnp.mean(values * values, axis=-1, keepdims=True)
        values = values * lax.rsqrt(mean_square + EPSILON) * gain
        values = values * cos_ref[...] + pltpu.roll(values, HD // 2, 1) * sin_ref[...]
        return values.astype(jnp.bfloat16).astype(jnp.float32)

    total = jnp.int32(0)
    for row in range(rows):
        start_ref[row] = total
        total = total + length_ref[0, row]
    start_ref[rows] = total

    query_gain = query_gain_ref[...]
    key_gain = key_gain_ref[...]
    for kv in range(kv_count):
        columns = slice(kv * HD, (kv + 1) * HD)
        new_keys[:, columns] = turned(head(heads + kv), key_gain)
        new_values[:, columns] = head(heads + kv_count + kv)
    for index in range(heads):
        queries[pl.ds(index, rows, stride=heads), :] = turned(head(index), query_gain)

    place = lax.broadcasted_iota(jnp.int32, (WINDOW + ALIGN, heads), 0)
    kv_of_row = lax.broadcasted_iota(jnp.int32, (heads, HD), 0) // group

    def with_new(ref, window, fresh, row):
        new = jnp.broadcast_to(fresh[pl.ds(row, 1), :], (ALIGN, fresh.shape[1]))
        return jnp.concatenate([ref[window, :], new.astype(jnp.bfloat16)], axis=0)

    def window_of(row):
        first, last = start_ref[row], start_ref[row + 1]
        base = jnp.minimum(first // ALIGN * ALIGN, pool - WINDOW)
        return first - base, last - base, pl.ds(pl.multiple_of(base, ALIGN), WINDOW)

    def rows_of(row):
        return pl.ds(pl.multiple_of(row * heads, heads), heads)

    def scored(row):
        first, last, window = window_of(row)
        query = queries[rows_of(row), :]
        spread = jnp.concatenate(
            [jnp.where(kv_of_row == kv, query, 0.0) for kv in range(kv_count)], axis=1
        ).astype(jnp.bfloat16)
        scores = lax.dot_general(
            with_new(key_ref, window, new_keys, row),
            spread,
            (((1,), (1,)), ((), ())),
            preferred_element_type=jnp.float32,
        )
        inside = ((place >= first) & (place < last)) | (place == WINDOW)
        return jnp.where(inside, scores * scale, -1e30)

    def weighed(scores):
        raised = jnp.exp2(scores - jnp.max(scores, axis=0, keepdims=True))
        weights = raised * (1.0 / jnp.sum(raised, axis=0, keepdims=True))
        return weights.astype(jnp.bfloat16)

    def mix(row, weights):
        mixed = lax.dot_general(
            weights,
            with_new(value_ref, window_of(row)[2], new_values, row),
            (((0,), (0,)), ((), ())),
            preferred_element_type=jnp.float32,
        )
        results[rows_of(row), :] = jnp.concatenate(
            [
                mixed[kv * group : (kv + 1) * group, kv * HD : (kv + 1) * HD]
                for kv in range(kv_count)
            ],
            axis=0,
        )

    def body(step, carry):
        at = [step * UNROLL + inner for inner in range(UNROLL)]
        weights = [weighed(scores) for scores in [scored(row) for row in at]]
        for row, weight in zip(at, weights):
            mix(row, weight)
        return carry

    lax.fori_loop(0, rows // UNROLL, body, 0)
    out_heads = out_ref.shape[2] // HD
    for index in range(heads):
        block, slot = index // out_heads, index % out_heads
        out_ref[block, :, slot * HD : (slot + 1) * HD] = results[
            pl.ds(index, rows, stride=heads), :
        ].astype(jnp.bfloat16)


def attend(merged, lengths, query_gain, key_gain, keys, values, count, swapped):
    rows = merged.shape[1]
    kv_count = keys.shape[1] // HD
    heads = merged.shape[0] * merged.shape[2] // HD - 2 * kv_count
    position = lengths.reshape(rows)
    frequency = ROPE_BASE ** (-jnp.arange(HD // 2, dtype=jnp.float32) * 2.0 / HD)
    angles = position.astype(jnp.float32)[:, None] * frequency[None, :]
    cosine, sine = jnp.cos(angles), jnp.sin(angles)
    return call(
        functools.partial(attention_kernel, kv_count),
        jax.ShapeDtypeStruct((count, rows, heads * HD // count), jnp.bfloat16),
        [SMEM] + [VMEM] * 7 + [HBM] * len(swapped),
        (
            lengths,
            merged,
            jnp.concatenate([cosine, cosine], axis=1),
            jnp.concatenate([-sine, sine], axis=1),
            query_gain[None, :],
            key_gain[None, :],
            keys,
            values,
            *swapped,
        ),
        [
            pltpu.VMEM((heads * rows, HD), jnp.float32),
            pltpu.VMEM((heads * rows, HD), jnp.float32),
            pltpu.VMEM((rows, kv_count * HD), jnp.float32),
            pltpu.VMEM((rows, kv_count * HD), jnp.float32),
            pltpu.SMEM((rows + 1,), jnp.int32),
        ],
        12,
        "ragged_attention",
    )


def on_device(
    hidden,
    lengths,
    key_cache,
    value_cache,
    expert_ids,
    gate_codes,
    expert_device,
    attention_gain,
    mixture_gain,
    query_gain,
    key_gain,
    project_weight,
    output_weight,
    expert_gate_up,
    expert_down,
):
    count, subs = lax.axis_size("dev"), lax.axis_size("sub")
    ring = Ring(count)
    rows, width = hidden.shape
    slots = expert_device.shape[0]

    gate_ups, downs = [], []
    for shift in range(1, subs):
        swap = [(i, (i - shift) % subs) for i in range(subs)]
        gate_ups.append(lax.ppermute(expert_gate_up[0], "sub", swap))
        downs.append(lax.ppermute(expert_down[0], "sub", swap))

    bf16 = jnp.bfloat16
    owners = ring.owners()
    dma = pltpu.SemaphoreType.DMA
    digits = call(
        digit_kernel,
        jax.ShapeDtypeStruct((rows, HD), bf16),
        [SMEM, VMEM, VMEM],
        (expert_device[None, :], expert_ids, gate_codes),
        [],
        4,
        "gate_digits",
    )
    normed = call(
        norm_kernel,
        jax.ShapeDtypeStruct((rows, width), bf16),
        [ANY] * 2,
        (hidden, attention_gain[None, :]),
        [pltpu.VMEM((rows, width), bf16), pltpu.VMEM((1, width), jnp.float32), dma((2,))],
        4,
        "attention_norm",
    )
    columns = project_weight.shape[1]
    gathered, pieces = ring_gather(ring, normed)
    (project_weight,) = loaded([project_weight], pieces[1], 50, "load_project")
    blocks = call(
        functools.partial(project_kernel, count),
        jax.ShapeDtypeStruct((count, rows, columns), bf16),
        [SMEM, VMEM, VMEM],
        (owners, gathered, project_weight),
        [],
        8,
        "project",
    )
    keys, values = loaded([key_cache[0], value_cache[0]], blocks, 44, "load_caches")
    blocks = lax.all_to_all(blocks, "dev", split_axis=0, concat_axis=0, tiled=True)
    if columns % HD:
        blocks = jnp.transpose(blocks, (1, 0, 2)).reshape(1, rows, -1)
    attention = attend(
        blocks, lengths, query_gain, key_gain, keys, values, count, [digits, *gate_ups, *downs]
    )
    features = lax.all_to_all(attention, "dev", split_axis=0, concat_axis=0, tiled=True)
    (output_weight,) = loaded([output_weight], attention, 44, "load_output")
    own, *partial = call(
        functools.partial(output_kernel, count),
        block_shapes(count, rows, width),
        [SMEM, VMEM, VMEM],
        (owners, features, output_weight),
        [pltpu.VMEM((count * rows, output_weight.shape[0]), bf16)],
        8,
        "output_projection",
    )
    up, down = ring_scatter_sum(ring, *partial)
    residual, sent = call(
        residual_kernel,
        [
            jax.ShapeDtypeStruct((rows, width), jnp.float32),
            jax.ShapeDtypeStruct((rows, width + HD), bf16),
        ],
        [VMEM] * 6,
        (hidden, own, up, down, mixture_gain[None, :], digits),
        [],
        4,
        "residual_norm",
    )
    shifts = jnp.arange(subs, dtype=jnp.int32)[None, :]
    own_slots = lax.axis_index("dev") * subs + (lax.axis_index("sub") + shifts) % subs
    gathered, pieces = ring_gather(ring, sent)
    (own_gate_up,) = loaded([expert_gate_up[0]], pieces[1], 42, "load_gate_up")
    (own_down,) = loaded([expert_down[0]], pieces[3], 42, "load_down")
    own, *partial = call(
        functools.partial(expert_kernel, count, slots),
        block_shapes(count, rows, width),
        [SMEM] + [VMEM] * (1 + 2 * subs),
        (own_slots, gathered, own_gate_up, *gate_ups, own_down, *downs),
        [
            pltpu.VMEM((count * rows, expert_down.shape[1]), bf16),
            pltpu.VMEM((count * rows, width), jnp.float32),
        ],
        18,
        "experts",
    )
    up, down = ring_scatter_sum(ring, *partial)
    return (residual + own + up + down).astype(bf16)


def solution(mesh):
    return jax.shard_map(
        on_device,
        mesh=mesh,
        in_specs=(
            P(("groups", "dev", "sub"), None),
            P(("groups", "dev", "sub"), None),
            P(("groups", "dev", "sub"), None, None),
            P(("groups", "dev", "sub"), None, None),
            P(("groups", "dev", "sub"), None),
            P(("groups", "dev", "sub"), None),
            P(),
            P(),
            P(),
            P(),
            P(),
            P(None, "dev"),
            P("dev", None),
            P(("dev", "sub"), None, None),
            P(("dev", "sub"), None, None),
        ),
        out_specs=P(("groups", "dev", "sub"), None),
        check_vma=False,
    )
```

```python
import functools
import math

import jax
import jax.numpy as jnp
from jax import lax
from jax.experimental import pallas as pl
from jax.experimental.pallas import tpu as pltpu
from jax.sharding import PartitionSpec as P

HD = 128

EPSILON = 1e-06
ROPE_BASE = 1000000.0
LOG2E = 1.4426950408889634
LONGEST = 256
ALIGN = 16
WINDOW = LONGEST + ALIGN
UNROLL = 8
TILE = 256


def norm_scale(values, scale_gain):
    mean_square = jnp.mean(values * values, axis=-1, keepdims=True)
    return values * lax.rsqrt(mean_square + EPSILON) * scale_gain


def ring_order(count):
    return list(range(0, count, 2)) + list(range(1, count, 2))[::-1]


class Ring:
    def __init__(self, count):
        self.count = count
        self.far = count // 2
        order = ring_order(count)
        self.forward = [(order[i], order[(i + 1) % count]) for i in range(count)]
        self.backward = [(b, a) for a, b in self.forward]
        self.distances = [0]
        for step in range(1, self.far):
            self.distances += [step, -step]
        self.distances += [self.far]

    def ahead(self, values):
        return lax.ppermute(values, "dev", self.forward)

    def behind(self, values):
        return lax.ppermute(values, "dev", self.backward)

    def owners(self):
        count = self.count
        device = lax.axis_index("dev").astype(jnp.int32)
        index = lax.broadcasted_iota(jnp.int32, (1, count), 1)
        step = (index + 1) // 2
        distance = jnp.where(index % 2 == 1, step, -step)
        place = jnp.where(device % 2 == 0, device // 2, count - 1 - device // 2)
        place = place + distance
        place = jnp.where(place < 0, place + count, place)
        place = jnp.where(place >= count, place - count, place)
        return jnp.where(place < self.far, 2 * place, 2 * (count - 1 - place) + 1)


def ring_gather(ring, block):
    half_rows = block.shape[0] // 2
    up, down = block, block
    pieces = [block]
    for step in range(1, ring.far):
        up, down = ring.ahead(up), ring.behind(down)
        pieces += [down, up]
    pieces += [ring.ahead(up[:half_rows]), ring.behind(down[half_rows:])]
    return jnp.concatenate(pieces, axis=0), pieces


def ring_scatter_sum(ring, far_up, far_down, ups, downs):
    half_width = far_up.shape[1]
    sent = jnp.bfloat16
    up, down = ring.ahead(far_up), ring.behind(far_down)
    for distance in range(ring.far - 1, 0, -1):
        mine_up, mine_down = ups[distance - 1], downs[distance - 1]
        up, down = up.astype(jnp.float32), down.astype(jnp.float32)
        if distance == ring.far - 1:
            up = jnp.concatenate([mine_up[:, :half_width] + up, mine_up[:, half_width:]], axis=1)
            down = jnp.concatenate(
                [mine_down[:, :half_width], mine_down[:, half_width:] + down], axis=1
            )
        else:
            up, down = mine_up + up, mine_down + down
        up, down = ring.ahead(up.astype(sent)), ring.behind(down.astype(sent))
    return up, down


def whole_blocks(kinds):
    return [pl.BlockSpec(memory_space=kind) for kind in kinds]


def call(body, outs, ins, operands, scratch, limit, name, cost=100):
    return pl.pallas_call(
        body,
        out_shape=outs,
        in_specs=whole_blocks(ins),
        out_specs=jax.tree.map(lambda _: pl.BlockSpec(memory_space=pltpu.VMEM), outs),
        scratch_shapes=scratch,
        cost_estimate=pl.CostEstimate(
            flops=0, bytes_accessed=cost * 1024 * 1024, transcendentals=0
        ),
        compiler_params=pltpu.CompilerParams(vmem_limit_bytes=limit * 1024 * 1024),
        name=name,
    )(*operands)


VMEM, SMEM, HBM, ANY = pltpu.VMEM, pltpu.SMEM, pltpu.HBM, pl.ANY


def start_copies(pairs, sems):
    copies = [
        pltpu.make_async_copy(source, target, sems.at[index])
        for index, (source, target) in enumerate(pairs)
    ]
    for copy in copies:
        copy.start()
    return copies


def digit_kernel(holder_ref, ids_ref, codes_ref, out_ref):
    ids, codes = ids_ref[...], codes_ref[...]
    lane = lax.broadcasted_iota(jnp.int32, out_ref.shape, 1)
    high = jnp.zeros(out_ref.shape, jnp.float32)
    for expert in range(holder_ref.shape[1]):
        code = jnp.sum(jnp.where(ids == expert, codes, 0), axis=1, keepdims=True)
        slot = holder_ref[0, expert]
        high = high + jnp.where(lane == slot, (code >> 5).astype(jnp.float32), 0.0)
        high = high + jnp.where(lane == slot + HD // 2, (code & 31).astype(jnp.float32), 0.0)
    out_ref[...] = high.astype(jnp.bfloat16)


def tiled_gain(gain):
    return jnp.broadcast_to(gain[None, :], (8, gain.shape[0]))


def load_kernel(number, *refs):
    sources, targets, sems = refs[:number], refs[-1 - number : -1], refs[-1]
    for copy in start_copies(list(zip(sources, targets)), sems):
        copy.wait()


def loaded(arrays, after, limit, name):
    number = len(arrays)
    return call(
        functools.partial(load_kernel, number),
        [jax.ShapeDtypeStruct(array.shape, array.dtype) for array in arrays],
        [HBM] * number + [ANY],
        (*arrays, after),
        [pltpu.SemaphoreType.DMA((number,))],
        limit,
        name,
    )


def project_kernel(count, owner_ref, hidden_ref, gain_ref, weight_ref, out_ref, held):
    rows = hidden_ref.shape[0] // count
    gain = gain_ref[:1, :]
    for index in range(count):
        at = slice(index * rows, (index + 1) * rows)
        values = hidden_ref[at, :].astype(jnp.float32)
        held[at, :] = norm_scale(values, gain).astype(jnp.bfloat16)
    product = jnp.dot(held[...], weight_ref[...], preferred_element_type=jnp.float32)
    product = product.astype(jnp.bfloat16)
    for index in range(count):
        out_ref[owner_ref[0, index]] = product[index * rows : (index + 1) * rows]


def output_kernel(count, owner_ref, feature_ref, weight_ref, *refs):
    outs, held = refs[:-1], refs[-1]
    rows = feature_ref.shape[1]
    for index in range(count):
        held[index * rows : (index + 1) * rows, :] = feature_ref[owner_ref[0, index]]
    product = jnp.dot(held[...], weight_ref[...], preferred_element_type=jnp.float32)
    split_blocks(count, rows, product, outs)


def split_blocks(count, rows, product, outs):
    own, far_up, far_down, ups, downs = outs
    half_width = product.shape[1] // 2
    own[...] = product[:rows]
    for index in range(1, count - 1):
        side = ups if index % 2 else downs
        side[(index - 1) // 2] = product[index * rows : (index + 1) * rows]
    last = product[(count - 1) * rows :].astype(jnp.bfloat16)
    far_up[...] = last[:, :half_width]
    far_down[...] = last[:, half_width:]


def block_shapes(count, rows, width):
    own = jax.ShapeDtypeStruct((rows, width), jnp.float32)
    half = jax.ShapeDtypeStruct((rows, width // 2), jnp.bfloat16)
    side = jax.ShapeDtypeStruct((count // 2 - 1, rows, width), jnp.float32)
    return [own, half, half, side, side]


def residual_kernel(
    hidden_ref, own_ref, up_ref, down_ref, gain_ref, digit_ref, residual_ref, sent_ref
):
    width = hidden_ref.shape[1]
    summed = own_ref[...] + up_ref[...].astype(jnp.float32) + down_ref[...].astype(jnp.float32)
    residual = hidden_ref[...].astype(jnp.float32) + summed
    residual_ref[...] = residual
    sent_ref[:, :width] = norm_scale(residual, gain_ref[:1, :]).astype(jnp.bfloat16)
    sent_ref[:, width:] = digit_ref[...]


def expert_kernel(count, slots, slot_ref, held, *refs):
    subs = slot_ref.shape[1]
    gate_ups, downs, refs = refs[:subs], refs[subs : 2 * subs], refs[2 * subs :]
    outs, (units, total) = refs[:5], refs[5:]
    width = total.shape[1]
    inner = units.shape[1]
    rows = held.shape[0] // count
    digits = held[:, width:].astype(jnp.float32)
    lane = lax.broadcasted_iota(jnp.int32, digits.shape, 1)
    codes = digits * 32.0 + pltpu.roll(digits, HD // 2, 1)
    codes = jnp.where(lane < slots, codes, 0.0)
    whole = jnp.sum(codes, axis=1, keepdims=True)
    for shift in range(subs):
        mine = jnp.where(lane == slot_ref[0, shift], codes, 0.0)
        weight = jnp.sum(mine, axis=1, keepdims=True) / whole
        for start in range(0, inner, TILE):
            gate, up = [
                jnp.dot(
                    held[:, :width],
                    gate_ups[shift][:, column : column + TILE],
                    preferred_element_type=jnp.float32,
                )
                for column in (start, inner + start)
            ]
            units[:, start : start + TILE] = (jax.nn.silu(gate) * up).astype(jnp.bfloat16)
        for start in range(0, width, 2 * TILE):
            columns = slice(start, start + 2 * TILE)
            result = jnp.dot(
                units[...], downs[shift][:, columns], preferred_element_type=jnp.float32
            )
            result = result.astype(jnp.bfloat16).astype(jnp.float32) * weight
            if shift:
                result = result + total[:, columns]
            total[:, columns] = result
    split_blocks(count, rows, total, outs)


def attention_kernel(
    kv_count,
    length_ref,
    merged_ref,
    cos_ref,
    sin_ref,
    query_gain_ref,
    key_gain_ref,
    key_hbm,
    value_hbm,
    *refs,
):
    out_ref, queries, results, new_keys, new_values, key_ref, value_ref, start_ref, sems = refs[-9:]
    fetches = [
        pltpu.make_async_copy(key_hbm, key_ref, sems.at[0]),
        pltpu.make_async_copy(value_hbm, value_ref, sems.at[1]),
    ]
    fetches[0].start()
    rows = merged_ref.shape[1]
    heads = queries.shape[0] // rows
    group = heads // kv_count
    pool = key_ref.shape[0]
    per_block = merged_ref.shape[2] // HD
    scale = LOG2E / math.sqrt(HD)

    def head(index):
        block, slot = index // per_block, index % per_block
        return merged_ref[block, :, slot * HD : (slot + 1) * HD].astype(jnp.float32)

    def turned(values, gain):
        mean_square = jnp.mean(values * values, axis=-1, keepdims=True)
        values = values * lax.rsqrt(mean_square + EPSILON) * gain
        values = values * cos_ref[...] + pltpu.roll(values, HD // 2, 1) * sin_ref[...]
        return values.astype(jnp.bfloat16).astype(jnp.float32)

    total = jnp.int32(0)
    for row in range(rows):
        start_ref[row] = total
        total = total + length_ref[0, row]
    start_ref[rows] = total

    query_gain = query_gain_ref[...]
    key_gain = key_gain_ref[...]
    for kv in range(kv_count):
        columns = slice(kv * HD, (kv + 1) * HD)
        new_keys[:, columns] = turned(head(heads + kv), key_gain)
        new_values[:, columns] = head(heads + kv_count + kv)
    for index in range(heads):
        if index == heads // 2:
            fetches[1].start()
        queries[pl.ds(index, rows, stride=heads), :] = turned(head(index), query_gain)

    fetches[0].wait()

    place = lax.broadcasted_iota(jnp.int32, (WINDOW + ALIGN, heads), 0)
    kv_of_row = lax.broadcasted_iota(jnp.int32, (heads, HD), 0) // group

    def with_new(ref, window, fresh, row):
        new = jnp.broadcast_to(fresh[pl.ds(row, 1), :], (ALIGN, fresh.shape[1]))
        return jnp.concatenate([ref[window, :], new.astype(jnp.bfloat16)], axis=0)

    def window_of(row):
        first, last = start_ref[row], start_ref[row + 1]
        base = jnp.minimum(first // ALIGN * ALIGN, pool - WINDOW)
        return first - base, last - base, pl.ds(pl.multiple_of(base, ALIGN), WINDOW)

    def rows_of(row):
        return pl.ds(pl.multiple_of(row * heads, heads), heads)

    def scored(row):
        first, last, window = window_of(row)
        query = queries[rows_of(row), :]
        spread = jnp.concatenate(
            [jnp.where(kv_of_row == kv, query, 0.0) for kv in range(kv_count)], axis=1
        ).astype(jnp.bfloat16)
        scores = lax.dot_general(
            with_new(key_ref, window, new_keys, row),
            spread,
            (((1,), (1,)), ((), ())),
            preferred_element_type=jnp.float32,
        )
        inside = ((place >= first) & (place < last)) | (place == WINDOW)
        return jnp.where(inside, scores * scale, -1e30)

    def weighed(scores):
        raised = jnp.exp2(scores - jnp.max(scores, axis=0, keepdims=True))
        weights = raised * (1.0 / jnp.sum(raised, axis=0, keepdims=True))
        return weights.astype(jnp.bfloat16)

    def mix(row, weights):
        mixed = lax.dot_general(
            weights,
            with_new(value_ref, window_of(row)[2], new_values, row),
            (((0,), (0,)), ((), ())),
            preferred_element_type=jnp.float32,
        )
        results[rows_of(row), :] = jnp.concatenate(
            [
                mixed[kv * group : (kv + 1) * group, kv * HD : (kv + 1) * HD]
                for kv in range(kv_count)
            ],
            axis=0,
        )

    def body(step, carry):
        at = [step * UNROLL + inner for inner in range(UNROLL)]
        weights = [weighed(scores) for scores in [scored(row) for row in at]]

        @pl.when(step == 0)
        def _():
            fetches[1].wait()

        for row, weight in zip(at, weights):
            mix(row, weight)
        return carry

    lax.fori_loop(0, rows // UNROLL, body, 0)
    out_heads = out_ref.shape[2] // HD
    for index in range(heads):
        block, slot = index // out_heads, index % out_heads
        out_ref[block, :, slot * HD : (slot + 1) * HD] = results[
            pl.ds(index, rows, stride=heads), :
        ].astype(jnp.bfloat16)


def attend(merged, lengths, query_gain, key_gain, keys, values, count, swapped):
    rows = merged.shape[1]
    kv_count = keys.shape[1] // HD
    heads = merged.shape[0] * merged.shape[2] // HD - 2 * kv_count
    position = lengths.reshape(rows)
    frequency = ROPE_BASE ** (-jnp.arange(HD // 2, dtype=jnp.float32) * 2.0 / HD)
    angles = position.astype(jnp.float32)[:, None] * frequency[None, :]
    cosine, sine = jnp.cos(angles), jnp.sin(angles)
    return call(
        functools.partial(attention_kernel, kv_count),
        jax.ShapeDtypeStruct((count, rows, heads * HD // count), jnp.bfloat16),
        [SMEM] + [VMEM] * 5 + [HBM] * (2 + len(swapped)),
        (
            lengths,
            merged,
            jnp.concatenate([cosine, cosine], axis=1),
            jnp.concatenate([-sine, sine], axis=1),
            query_gain[None, :],
            key_gain[None, :],
            keys,
            values,
            *swapped,
        ),
        [
            pltpu.VMEM((heads * rows, HD), jnp.float32),
            pltpu.VMEM((heads * rows, HD), jnp.float32),
            pltpu.VMEM((rows, kv_count * HD), jnp.float32),
            pltpu.VMEM((rows, kv_count * HD), jnp.float32),
            pltpu.VMEM(keys.shape, keys.dtype),
            pltpu.VMEM(values.shape, values.dtype),
            pltpu.SMEM((rows + 1,), jnp.int32),
            pltpu.SemaphoreType.DMA((2,)),
        ],
        57,
        "ragged_attention",
    )


def on_device(
    hidden,
    lengths,
    key_cache,
    value_cache,
    expert_ids,
    gate_codes,
    expert_device,
    attention_gain,
    mixture_gain,
    query_gain,
    key_gain,
    project_weight,
    output_weight,
    expert_gate_up,
    expert_down,
):
    count, subs = lax.axis_size("dev"), lax.axis_size("sub")
    ring = Ring(count)
    rows, width = hidden.shape
    slots = expert_device.shape[0]

    gate_ups, downs = [], []
    for shift in range(1, subs):
        swap = [(i, (i - shift) % subs) for i in range(subs)]
        gate_ups.append(lax.ppermute(expert_gate_up[0], "sub", swap))
        downs.append(lax.ppermute(expert_down[0], "sub", swap))

    bf16 = jnp.bfloat16
    owners = ring.owners()
    dma = pltpu.SemaphoreType.DMA
    digits = call(
        digit_kernel,
        jax.ShapeDtypeStruct((rows, HD), bf16),
        [SMEM, VMEM, VMEM],
        (expert_device[None, :], expert_ids, gate_codes),
        [],
        4,
        "gate_digits",
    )
    columns = project_weight.shape[1]
    gathered, pieces = ring_gather(ring, hidden)
    (project_weight,) = loaded([project_weight], pieces[1], 50, "load_project")
    blocks = call(
        functools.partial(project_kernel, count),
        jax.ShapeDtypeStruct((count, rows, columns), bf16),
        [SMEM, VMEM, VMEM, VMEM],
        (owners, gathered, tiled_gain(attention_gain), project_weight),
        [pltpu.VMEM((count * rows, width), bf16)],
        8,
        "project",
    )
    blocks = lax.all_to_all(blocks, "dev", split_axis=0, concat_axis=0, tiled=True)
    if columns % HD:
        blocks = jnp.transpose(blocks, (1, 0, 2)).reshape(1, rows, -1)
    attention = attend(
        blocks, lengths, query_gain, key_gain, key_cache[0], value_cache[0], count, [digits, *gate_ups, *downs]
    )
    features = lax.all_to_all(attention, "dev", split_axis=0, concat_axis=0, tiled=True)
    (output_weight,) = loaded([output_weight], attention, 44, "load_output")
    own, *partial = call(
        functools.partial(output_kernel, count),
        block_shapes(count, rows, width),
        [SMEM, VMEM, VMEM],
        (owners, features, output_weight),
        [pltpu.VMEM((count * rows, output_weight.shape[0]), bf16)],
        8,
        "output_projection",
    )
    up, down = ring_scatter_sum(ring, *partial)
    residual, sent = call(
        residual_kernel,
        [
            jax.ShapeDtypeStruct((rows, width), jnp.float32),
            jax.ShapeDtypeStruct((rows, width + HD), bf16),
        ],
        [VMEM] * 6,
        (hidden, own, up, down, tiled_gain(mixture_gain), digits),
        [],
        4,
        "residual_norm",
    )
    shifts = jnp.arange(subs, dtype=jnp.int32)[None, :]
    own_slots = lax.axis_index("dev") * subs + (lax.axis_index("sub") + shifts) % subs
    gathered, pieces = ring_gather(ring, sent)
    weights = []
    for index, gate_up in enumerate([expert_gate_up[0]] + gate_ups):
        weights += loaded([gate_up], pieces[2 * index + 1], 4, "load_gate_up")
    weights += loaded([expert_down[0]] + downs, pieces[2 * subs + 1], 4, "load_downs")
    own, *partial = call(
        functools.partial(expert_kernel, count, slots),
        block_shapes(count, rows, width),
        [SMEM] + [VMEM] * (1 + 2 * subs),
        (own_slots, gathered, *weights),
        [
            pltpu.VMEM((count * rows, expert_down.shape[1]), bf16),
            pltpu.VMEM((count * rows, width), jnp.float32),
        ],
        18,
        "experts",
    )
    up, down = ring_scatter_sum(ring, *partial)
    return (residual + own + up + down).astype(bf16)


def solution(mesh):
    return jax.shard_map(
        on_device,
        mesh=mesh,
        in_specs=(
            P(("groups", "dev", "sub"), None),
            P(("groups", "dev", "sub"), None),
            P(("groups", "dev", "sub"), None, None),
            P(("groups", "dev", "sub"), None, None),
            P(("groups", "dev", "sub"), None),
            P(("groups", "dev", "sub"), None),
            P(),
            P(),
            P(),
            P(),
            P(),
            P(None, "dev"),
            P("dev", None),
            P(("dev", "sub"), None, None),
            P(("dev", "sub"), None, None),
        ),
        out_specs=P(("groups", "dev", "sub"), None),
        check_vma=False,
    )
```

```python
import functools
import math

import jax
import jax.numpy as jnp
from jax import lax
from jax.experimental import pallas as pl
from jax.experimental.pallas import tpu as pltpu
from jax.sharding import PartitionSpec as P

HD = 128

EPSILON = 1e-06
ROPE_BASE = 1000000.0
LOG2E = 1.4426950408889634
LONGEST = 256
ALIGN = 16
WINDOW = LONGEST + ALIGN
UNROLL = 8
TILE = 256


def norm_scale(values, scale_gain):
    mean_square = jnp.mean(values * values, axis=-1, keepdims=True)
    return values * lax.rsqrt(mean_square + EPSILON) * scale_gain


def ring_order(count):
    return list(range(0, count, 2)) + list(range(1, count, 2))[::-1]


class Ring:
    def __init__(self, count):
        self.count = count
        self.far = count // 2
        order = ring_order(count)
        self.forward = [(order[i], order[(i + 1) % count]) for i in range(count)]
        self.backward = [(b, a) for a, b in self.forward]
        self.distances = [0]
        for step in range(1, self.far):
            self.distances += [step, -step]
        self.distances += [self.far]

    def ahead(self, values):
        return lax.ppermute(values, "dev", self.forward)

    def behind(self, values):
        return lax.ppermute(values, "dev", self.backward)

    def owners(self):
        count = self.count
        device = lax.axis_index("dev").astype(jnp.int32)
        index = lax.broadcasted_iota(jnp.int32, (1, count), 1)
        step = (index + 1) // 2
        distance = jnp.where(index % 2 == 1, step, -step)
        place = jnp.where(device % 2 == 0, device // 2, count - 1 - device // 2)
        place = place + distance
        place = jnp.where(place < 0, place + count, place)
        place = jnp.where(place >= count, place - count, place)
        return jnp.where(place < self.far, 2 * place, 2 * (count - 1 - place) + 1)


def ring_gather(ring, block):
    half_rows = block.shape[0] // 2
    up, down = block, block
    pieces = [block]
    for step in range(1, ring.far):
        up, down = ring.ahead(up), ring.behind(down)
        pieces += [down, up]
    pieces += [ring.ahead(up[:half_rows]), ring.behind(down[half_rows:])]
    return jnp.concatenate(pieces, axis=0), pieces


def ring_scatter_sum(ring, far_up, far_down, ups, downs):
    half_width = far_up.shape[1]
    sent = jnp.bfloat16
    up, down = ring.ahead(far_up), ring.behind(far_down)
    for distance in range(ring.far - 1, 0, -1):
        mine_up, mine_down = ups[distance - 1], downs[distance - 1]
        up, down = up.astype(jnp.float32), down.astype(jnp.float32)
        if distance == ring.far - 1:
            up = jnp.concatenate([mine_up[:, :half_width] + up, mine_up[:, half_width:]], axis=1)
            down = jnp.concatenate(
                [mine_down[:, :half_width], mine_down[:, half_width:] + down], axis=1
            )
        else:
            up, down = mine_up + up, mine_down + down
        up, down = ring.ahead(up.astype(sent)), ring.behind(down.astype(sent))
        if distance == 2:
            early = up
    return up, down, early


def whole_blocks(kinds):
    return [pl.BlockSpec(memory_space=kind) for kind in kinds]


def call(body, outs, ins, operands, scratch, limit, name, cost=100):
    return pl.pallas_call(
        body,
        out_shape=outs,
        in_specs=whole_blocks(ins),
        out_specs=jax.tree.map(lambda _: pl.BlockSpec(memory_space=pltpu.VMEM), outs),
        scratch_shapes=scratch,
        cost_estimate=pl.CostEstimate(
            flops=0, bytes_accessed=cost * 1024 * 1024, transcendentals=0
        ),
        compiler_params=pltpu.CompilerParams(vmem_limit_bytes=limit * 1024 * 1024),
        name=name,
    )(*operands)


VMEM, SMEM, HBM, ANY = pltpu.VMEM, pltpu.SMEM, pltpu.HBM, pl.ANY


def start_copies(pairs, sems):
    copies = [
        pltpu.make_async_copy(source, target, sems.at[index])
        for index, (source, target) in enumerate(pairs)
    ]
    for copy in copies:
        copy.start()
    return copies


def digit_kernel(holder_ref, ids_ref, codes_ref, out_ref):
    ids, codes = ids_ref[...], codes_ref[...]
    lane = lax.broadcasted_iota(jnp.int32, out_ref.shape, 1)
    high = jnp.zeros(out_ref.shape, jnp.float32)
    for expert in range(holder_ref.shape[1]):
        code = jnp.sum(jnp.where(ids == expert, codes, 0), axis=1, keepdims=True)
        slot = holder_ref[0, expert]
        high = high + jnp.where(lane == slot, (code >> 5).astype(jnp.float32), 0.0)
        high = high + jnp.where(lane == slot + HD // 2, (code & 31).astype(jnp.float32), 0.0)
    out_ref[...] = high.astype(jnp.bfloat16)


def tiled_gain(gain):
    return jnp.broadcast_to(gain[None, :], (8, gain.shape[0]))


def load_kernel(number, *refs):
    sources, targets, sems = refs[:number], refs[-1 - number : -1], refs[-1]
    for copy in start_copies(list(zip(sources, targets)), sems):
        copy.wait()


def loaded(arrays, after, limit, name):
    number = len(arrays)
    return call(
        functools.partial(load_kernel, number),
        [jax.ShapeDtypeStruct(array.shape, array.dtype) for array in arrays],
        [HBM] * number + [ANY],
        (*arrays, after),
        [pltpu.SemaphoreType.DMA((number,))],
        limit,
        name,
    )


def project(hidden_ref, gain_ref, weight_ref, held, rows):
    gain = gain_ref[:1, :]
    for start in range(0, hidden_ref.shape[0], rows):
        at = slice(start, start + rows)
        values = hidden_ref[at, :].astype(jnp.float32)
        held[at, :] = norm_scale(values, gain).astype(jnp.bfloat16)
    product = jnp.dot(held[...], weight_ref[...], preferred_element_type=jnp.float32)
    return product.astype(jnp.bfloat16)


def project_near_kernel(rows, hidden_ref, gain_ref, weight_ref, out_ref, held):
    out_ref[...] = project(hidden_ref, gain_ref, weight_ref, held, rows)


def project_kernel(count, owner_ref, near_ref, hidden_ref, gain_ref, weight_ref, *refs):
    out_ref, held = refs[-2:]
    rows = (near_ref.shape[0] + hidden_ref.shape[0]) // count
    nearby = near_ref.shape[0] // rows
    product = project(hidden_ref, gain_ref, weight_ref, held, rows)
    for index in range(nearby):
        out_ref[owner_ref[0, index]] = near_ref[index * rows : (index + 1) * rows, :]
    for index in range(nearby, count):
        at = (index - nearby) * rows
        out_ref[owner_ref[0, index]] = product[at : at + rows]


def output_kernel(count, owner_ref, feature_ref, weight_ref, *refs):
    outs, held = refs[:-1], refs[-1]
    rows = feature_ref.shape[1]
    for index in range(count):
        held[index * rows : (index + 1) * rows, :] = feature_ref[owner_ref[0, index]]
    product = jnp.dot(held[...], weight_ref[...], preferred_element_type=jnp.float32)
    split_blocks(count, rows, product, outs)


def split_blocks(count, rows, product, outs):
    own, far_up, far_down, ups, downs = outs
    half_width = product.shape[1] // 2
    own[...] = product[:rows]
    for index in range(1, count - 1):
        side = ups if index % 2 else downs
        side[(index - 1) // 2] = product[index * rows : (index + 1) * rows]
    last = product[(count - 1) * rows :].astype(jnp.bfloat16)
    far_up[...] = last[:, :half_width]
    far_down[...] = last[:, half_width:]


def block_shapes(count, rows, width):
    own = jax.ShapeDtypeStruct((rows, width), jnp.float32)
    half = jax.ShapeDtypeStruct((rows, width // 2), jnp.bfloat16)
    side = jax.ShapeDtypeStruct((count // 2 - 1, rows, width), jnp.float32)
    return [own, half, half, side, side]


def residual_kernel(
    hidden_ref, own_ref, up_ref, down_ref, gain_ref, digit_ref, residual_ref, sent_ref
):
    width = hidden_ref.shape[1]
    summed = own_ref[...] + up_ref[...].astype(jnp.float32) + down_ref[...].astype(jnp.float32)
    residual = hidden_ref[...].astype(jnp.float32) + summed
    residual_ref[...] = residual
    sent_ref[:, :width] = norm_scale(residual, gain_ref[:1, :]).astype(jnp.bfloat16)
    sent_ref[:, width:] = digit_ref[...]


def expert_kernel(count, slots, slot_ref, held, *refs):
    subs = slot_ref.shape[1]
    gate_ups, downs, refs = refs[:subs], refs[subs : 2 * subs], refs[2 * subs :]
    outs, (units, total) = refs[:5], refs[5:]
    width = total.shape[1]
    inner = units.shape[1]
    rows = held.shape[0] // count
    digits = held[:, width:].astype(jnp.float32)
    lane = lax.broadcasted_iota(jnp.int32, digits.shape, 1)
    codes = digits * 32.0 + pltpu.roll(digits, HD // 2, 1)
    codes = jnp.where(lane < slots, codes, 0.0)
    whole = jnp.sum(codes, axis=1, keepdims=True)
    for shift in range(subs):
        mine = jnp.where(lane == slot_ref[0, shift], codes, 0.0)
        weight = jnp.sum(mine, axis=1, keepdims=True) / whole
        for start in range(0, inner, TILE):
            gate, up = [
                jnp.dot(
                    held[:, :width],
                    gate_ups[shift][:, column : column + TILE],
                    preferred_element_type=jnp.float32,
                )
                for column in (start, inner + start)
            ]
            units[:, start : start + TILE] = (jax.nn.silu(gate) * up).astype(jnp.bfloat16)
        for start in range(0, width, 2 * TILE):
            columns = slice(start, start + 2 * TILE)
            result = jnp.dot(
                units[...], downs[shift][:, columns], preferred_element_type=jnp.float32
            )
            result = result.astype(jnp.bfloat16).astype(jnp.float32) * weight
            if shift:
                result = result + total[:, columns]
            total[:, columns] = result
    split_blocks(count, rows, total, outs)


def attention_kernel(
    kv_count,
    length_ref,
    merged_ref,
    cos_ref,
    sin_ref,
    query_gain_ref,
    key_gain_ref,
    key_hbm,
    value_hbm,
    *refs,
):
    out_ref, queries, results, new_keys, new_values, key_ref, value_ref, start_ref, sems = refs[-9:]
    fetches = [
        pltpu.make_async_copy(key_hbm, key_ref, sems.at[0]),
        pltpu.make_async_copy(value_hbm, value_ref, sems.at[1]),
    ]
    fetches[0].start()
    rows = merged_ref.shape[1]
    heads = queries.shape[0] // rows
    group = heads // kv_count
    pool = key_ref.shape[0]
    per_block = merged_ref.shape[2] // HD
    scale = LOG2E / math.sqrt(HD)

    def head(index):
        block, slot = index // per_block, index % per_block
        return merged_ref[block, :, slot * HD : (slot + 1) * HD].astype(jnp.float32)

    def turned(values, gain):
        mean_square = jnp.mean(values * values, axis=-1, keepdims=True)
        values = values * lax.rsqrt(mean_square + EPSILON) * gain
        values = values * cos_ref[...] + pltpu.roll(values, HD // 2, 1) * sin_ref[...]
        return values.astype(jnp.bfloat16).astype(jnp.float32)

    total = jnp.int32(0)
    for row in range(rows):
        start_ref[row] = total
        total = total + length_ref[0, row]
    start_ref[rows] = total

    query_gain = query_gain_ref[...]
    key_gain = key_gain_ref[...]
    for kv in range(kv_count):
        columns = slice(kv * HD, (kv + 1) * HD)
        new_keys[:, columns] = turned(head(heads + kv), key_gain)
        new_values[:, columns] = head(heads + kv_count + kv)
    for index in range(heads):
        if index == heads // 2:
            fetches[1].start()
        queries[pl.ds(index, rows, stride=heads), :] = turned(head(index), query_gain)

    fetches[0].wait()

    place = lax.broadcasted_iota(jnp.int32, (WINDOW + ALIGN, heads), 0)
    kv_of_row = lax.broadcasted_iota(jnp.int32, (heads, HD), 0) // group

    def with_new(ref, window, fresh, row):
        new = jnp.broadcast_to(fresh[pl.ds(row, 1), :], (ALIGN, fresh.shape[1]))
        return jnp.concatenate([ref[window, :], new.astype(jnp.bfloat16)], axis=0)

    def window_of(row):
        first, last = start_ref[row], start_ref[row + 1]
        base = jnp.minimum(first // ALIGN * ALIGN, pool - WINDOW)
        return first - base, last - base, pl.ds(pl.multiple_of(base, ALIGN), WINDOW)

    def rows_of(row):
        return pl.ds(pl.multiple_of(row * heads, heads), heads)

    def scored(row):
        first, last, window = window_of(row)
        query = queries[rows_of(row), :]
        spread = jnp.concatenate(
            [jnp.where(kv_of_row == kv, query, 0.0) for kv in range(kv_count)], axis=1
        ).astype(jnp.bfloat16)
        scores = lax.dot_general(
            with_new(key_ref, window, new_keys, row),
            spread,
            (((1,), (1,)), ((), ())),
            preferred_element_type=jnp.float32,
        )
        inside = ((place >= first) & (place < last)) | (place == WINDOW)
        return jnp.where(inside, scores * scale, -1e30)

    def weighed(scores):
        raised = jnp.exp2(scores - jnp.max(scores, axis=0, keepdims=True))
        weights = raised * (1.0 / jnp.sum(raised, axis=0, keepdims=True))
        return weights.astype(jnp.bfloat16)

    def mix(row, weights):
        mixed = lax.dot_general(
            weights,
            with_new(value_ref, window_of(row)[2], new_values, row),
            (((0,), (0,)), ((), ())),
            preferred_element_type=jnp.float32,
        )
        results[rows_of(row), :] = jnp.concatenate(
            [
                mixed[kv * group : (kv + 1) * group, kv * HD : (kv + 1) * HD]
                for kv in range(kv_count)
            ],
            axis=0,
        )

    def body(step, carry):
        at = [step * UNROLL + inner for inner in range(UNROLL)]
        weights = [weighed(scores) for scores in [scored(row) for row in at]]

        @pl.when(step == 0)
        def _():
            fetches[1].wait()

        for row, weight in zip(at, weights):
            mix(row, weight)
        return carry

    lax.fori_loop(0, rows // UNROLL, body, 0)
    out_heads = out_ref.shape[2] // HD
    for index in range(heads):
        block, slot = index // out_heads, index % out_heads
        out_ref[block, :, slot * HD : (slot + 1) * HD] = results[
            pl.ds(index, rows, stride=heads), :
        ].astype(jnp.bfloat16)


def attend(merged, lengths, query_gain, key_gain, keys, values, count, swapped):
    rows = merged.shape[1]
    kv_count = keys.shape[1] // HD
    heads = merged.shape[0] * merged.shape[2] // HD - 2 * kv_count
    position = lengths.reshape(rows)
    frequency = ROPE_BASE ** (-jnp.arange(HD // 2, dtype=jnp.float32) * 2.0 / HD)
    angles = position.astype(jnp.float32)[:, None] * frequency[None, :]
    cosine, sine = jnp.cos(angles), jnp.sin(angles)
    return call(
        functools.partial(attention_kernel, kv_count),
        jax.ShapeDtypeStruct((count, rows, heads * HD // count), jnp.bfloat16),
        [SMEM] + [VMEM] * 5 + [HBM] * (2 + len(swapped)),
        (
            lengths,
            merged,
            jnp.concatenate([cosine, cosine], axis=1),
            jnp.concatenate([-sine, sine], axis=1),
            query_gain[None, :],
            key_gain[None, :],
            keys,
            values,
            *swapped,
        ),
        [
            pltpu.VMEM((heads * rows, HD), jnp.float32),
            pltpu.VMEM((heads * rows, HD), jnp.float32),
            pltpu.VMEM((rows, kv_count * HD), jnp.float32),
            pltpu.VMEM((rows, kv_count * HD), jnp.float32),
            pltpu.VMEM(keys.shape, keys.dtype),
            pltpu.VMEM(values.shape, values.dtype),
            pltpu.SMEM((rows + 1,), jnp.int32),
            pltpu.SemaphoreType.DMA((2,)),
        ],
        57,
        "ragged_attention",
    )


def on_device(
    hidden,
    lengths,
    key_cache,
    value_cache,
    expert_ids,
    gate_codes,
    expert_device,
    attention_gain,
    mixture_gain,
    query_gain,
    key_gain,
    project_weight,
    output_weight,
    expert_gate_up,
    expert_down,
):
    count, subs = lax.axis_size("dev"), lax.axis_size("sub")
    ring = Ring(count)
    rows, width = hidden.shape
    slots = expert_device.shape[0]

    def swapped(values):
        return [
            lax.ppermute(values, "sub", [(i, (i - shift) % subs) for i in range(subs)])
            for shift in range(1, subs)
        ]

    gate_ups = swapped(expert_gate_up[0])

    bf16 = jnp.bfloat16
    owners = ring.owners()
    dma = pltpu.SemaphoreType.DMA
    digits = call(
        digit_kernel,
        jax.ShapeDtypeStruct((rows, HD), bf16),
        [SMEM, VMEM, VMEM],
        (expert_device[None, :], expert_ids, gate_codes),
        [],
        4,
        "gate_digits",
    )
    columns = project_weight.shape[1]
    _, pieces = ring_gather(ring, hidden)
    (project_weight,) = loaded([project_weight], pieces[1], 50, "load_project")
    gain = tiled_gain(attention_gain)
    nearby = max(1, count - 3)
    near = call(
        functools.partial(project_near_kernel, rows),
        jax.ShapeDtypeStruct((nearby * rows, columns), bf16),
        [VMEM] * 3,
        (jnp.concatenate(pieces[:nearby], axis=0), gain, project_weight),
        [pltpu.VMEM((nearby * rows, width), bf16)],
        8,
        "project_near",
    )
    late = jnp.concatenate(pieces[nearby:], axis=0)
    blocks = call(
        functools.partial(project_kernel, count),
        jax.ShapeDtypeStruct((count, rows, columns), bf16),
        [SMEM] + [VMEM] * 4,
        (owners, near, late, gain, project_weight),
        [pltpu.VMEM(late.shape, bf16)],
        8,
        "project",
    )
    blocks = lax.all_to_all(blocks, "dev", split_axis=0, concat_axis=0, tiled=True)
    if columns % HD:
        blocks = jnp.transpose(blocks, (1, 0, 2)).reshape(1, rows, -1)
    attention = attend(
        blocks, lengths, query_gain, key_gain, key_cache[0], value_cache[0], count, [digits, *gate_ups]
    )
    down, attention = lax.optimization_barrier((expert_down[0], attention))
    downs = swapped(down)
    features = lax.all_to_all(attention, "dev", split_axis=0, concat_axis=0, tiled=True)
    (output_weight,) = loaded([output_weight], attention, 44, "load_output")
    own, *partial = call(
        functools.partial(output_kernel, count),
        block_shapes(count, rows, width),
        [SMEM, VMEM, VMEM],
        (owners, features, output_weight),
        [pltpu.VMEM((count * rows, output_weight.shape[0]), bf16)],
        8,
        "output_projection",
    )
    up, down, early = ring_scatter_sum(ring, *partial)
    own_gate_up = loaded([expert_gate_up[0]], early, 4, "load_gate_up")
    residual, sent = call(
        residual_kernel,
        [
            jax.ShapeDtypeStruct((rows, width), jnp.float32),
            jax.ShapeDtypeStruct((rows, width + HD), bf16),
        ],
        [VMEM] * 6,
        (hidden, own, up, down, tiled_gain(mixture_gain), digits),
        [],
        4,
        "residual_norm",
    )
    shifts = jnp.arange(subs, dtype=jnp.int32)[None, :]
    own_slots = lax.axis_index("dev") * subs + (lax.axis_index("sub") + shifts) % subs
    gathered, pieces = ring_gather(ring, sent)
    weights = list(own_gate_up)
    for index, gate_up in enumerate(gate_ups):
        weights += loaded([gate_up], pieces[2 * index + 1], 4, "load_gate_up")
    weights += loaded([expert_down[0]], pieces[2 * subs - 1], 4, "load_down")
    weights = [*weights, *downs]
    own, *partial = call(
        functools.partial(expert_kernel, count, slots),
        block_shapes(count, rows, width),
        [SMEM] + [VMEM] * (1 + 2 * subs),
        (own_slots, gathered, *weights),
        [
            pltpu.VMEM((count * rows, expert_down.shape[1]), bf16),
            pltpu.VMEM((count * rows, width), jnp.float32),
        ],
        18,
        "experts",
    )
    up, down, _ = ring_scatter_sum(ring, *partial)
    return (residual + own + up + down).astype(bf16)


def solution(mesh):
    return jax.shard_map(
        on_device,
        mesh=mesh,
        in_specs=(
            P(("groups", "dev", "sub"), None),
            P(("groups", "dev", "sub"), None),
            P(("groups", "dev", "sub"), None, None),
            P(("groups", "dev", "sub"), None, None),
            P(("groups", "dev", "sub"), None),
            P(("groups", "dev", "sub"), None),
            P(),
            P(),
            P(),
            P(),
            P(),
            P(None, "dev"),
            P("dev", None),
            P(("dev", "sub"), None, None),
            P(("dev", "sub"), None, None),
        ),
        out_specs=P(("groups", "dev", "sub"), None),
        check_vma=False,
    )
```

```python
import functools
import math

import jax
import jax.numpy as jnp
from jax import lax
from jax.experimental import pallas as pl
from jax.experimental.pallas import tpu as pltpu
from jax.sharding import PartitionSpec as P

HD = 128

EPSILON = 1e-06
ROPE_BASE = 1000000.0
LOG2E = 1.4426950408889634
LONGEST = 256
ALIGN = 16
WINDOW = LONGEST + ALIGN
UNROLL = 16
TILE = 256


def norm_scale(values, scale_gain):
    mean_square = jnp.mean(values * values, axis=-1, keepdims=True)
    return values * lax.rsqrt(mean_square + EPSILON) * scale_gain


def ring_order(count):
    return list(range(0, count, 2)) + list(range(1, count, 2))[::-1]


class Ring:
    def __init__(self, count):
        self.count = count
        self.far = count // 2
        order = ring_order(count)
        self.forward = [(order[i], order[(i + 1) % count]) for i in range(count)]
        self.backward = [(b, a) for a, b in self.forward]
        self.distances = [0]
        for step in range(1, self.far):
            self.distances += [step, -step]
        self.distances += [self.far]

    def ahead(self, values):
        return lax.ppermute(values, "dev", self.forward)

    def behind(self, values):
        return lax.ppermute(values, "dev", self.backward)

    def owners(self):
        count = self.count
        device = lax.axis_index("dev").astype(jnp.int32)
        index = lax.broadcasted_iota(jnp.int32, (1, count), 1)
        step = (index + 1) // 2
        distance = jnp.where(index % 2 == 1, step, -step)
        place = jnp.where(device % 2 == 0, device // 2, count - 1 - device // 2)
        place = place + distance
        place = jnp.where(place < 0, place + count, place)
        place = jnp.where(place >= count, place - count, place)
        return jnp.where(place < self.far, 2 * place, 2 * (count - 1 - place) + 1)


def ring_gather(ring, block):
    half_rows = block.shape[0] // 2
    up, down = block, block
    pieces = [block]
    for step in range(1, ring.far):
        up, down = ring.ahead(up), ring.behind(down)
        pieces += [down, up]
    pieces += [ring.ahead(up[:half_rows]), ring.behind(down[half_rows:])]
    return jnp.concatenate(pieces, axis=0), pieces


def ring_scatter_sum(ring, far_up, far_down, ups, downs):
    half_width = far_up.shape[1]
    sent = jnp.bfloat16
    up, down = ring.ahead(far_up), ring.behind(far_down)
    for distance in range(ring.far - 1, 0, -1):
        mine_up, mine_down = ups[distance - 1], downs[distance - 1]
        up, down = up.astype(jnp.float32), down.astype(jnp.float32)
        if distance == ring.far - 1:
            up = jnp.concatenate([mine_up[:, :half_width] + up, mine_up[:, half_width:]], axis=1)
            down = jnp.concatenate(
                [mine_down[:, :half_width], mine_down[:, half_width:] + down], axis=1
            )
        else:
            up, down = mine_up + up, mine_down + down
        up, down = ring.ahead(up.astype(sent)), ring.behind(down.astype(sent))
        if distance == 2:
            early = up
    return up, down, early


def whole_blocks(kinds):
    return [pl.BlockSpec(memory_space=kind) for kind in kinds]


def call(body, outs, ins, operands, scratch, limit, name, cost=100):
    return pl.pallas_call(
        body,
        out_shape=outs,
        in_specs=whole_blocks(ins),
        out_specs=jax.tree.map(lambda _: pl.BlockSpec(memory_space=pltpu.VMEM), outs),
        scratch_shapes=scratch,
        cost_estimate=pl.CostEstimate(
            flops=0, bytes_accessed=cost * 1024 * 1024, transcendentals=0
        ),
        compiler_params=pltpu.CompilerParams(vmem_limit_bytes=limit * 1024 * 1024),
        name=name,
    )(*operands)


VMEM, SMEM, HBM, ANY = pltpu.VMEM, pltpu.SMEM, pltpu.HBM, pl.ANY


def start_copies(pairs, sems):
    copies = [
        pltpu.make_async_copy(source, target, sems.at[index])
        for index, (source, target) in enumerate(pairs)
    ]
    for copy in copies:
        copy.start()
    return copies


def digit_kernel(holder_ref, ids_ref, codes_ref, out_ref):
    ids, codes = ids_ref[...], codes_ref[...]
    lane = lax.broadcasted_iota(jnp.int32, out_ref.shape, 1)
    high = jnp.zeros(out_ref.shape, jnp.float32)
    for expert in range(holder_ref.shape[1]):
        code = jnp.sum(jnp.where(ids == expert, codes, 0), axis=1, keepdims=True)
        slot = holder_ref[0, expert]
        high = high + jnp.where(lane == slot, (code >> 5).astype(jnp.float32), 0.0)
        high = high + jnp.where(lane == slot + HD // 2, (code & 31).astype(jnp.float32), 0.0)
    out_ref[...] = high.astype(jnp.bfloat16)


def tiled_gain(gain):
    return jnp.broadcast_to(gain[None, :], (8, gain.shape[0]))


def load_kernel(number, *refs):
    sources, targets, sems = refs[:number], refs[-1 - number : -1], refs[-1]
    for copy in start_copies(list(zip(sources, targets)), sems):
        copy.wait()


def loaded(arrays, after, limit, name):
    number = len(arrays)
    return call(
        functools.partial(load_kernel, number),
        [jax.ShapeDtypeStruct(array.shape, array.dtype) for array in arrays],
        [HBM] * number + [ANY],
        (*arrays, after),
        [pltpu.SemaphoreType.DMA((number,))],
        limit,
        name,
    )


def project(hidden_ref, gain_ref, weight_ref, held, rows):
    gain = gain_ref[:1, :]
    for start in range(0, hidden_ref.shape[0], rows):
        at = slice(start, start + rows)
        values = hidden_ref[at, :].astype(jnp.float32)
        held[at, :] = norm_scale(values, gain).astype(jnp.bfloat16)
    product = jnp.dot(held[...], weight_ref[...], preferred_element_type=jnp.float32)
    return product.astype(jnp.bfloat16)


def project_near_kernel(rows, hidden_ref, gain_ref, weight_ref, out_ref, held):
    out_ref[...] = project(hidden_ref, gain_ref, weight_ref, held, rows)


def project_kernel(count, owner_ref, near_ref, hidden_ref, gain_ref, weight_ref, *refs):
    out_ref, held = refs[-2:]
    rows = (near_ref.shape[0] + hidden_ref.shape[0]) // count
    nearby = near_ref.shape[0] // rows
    product = project(hidden_ref, gain_ref, weight_ref, held, rows)
    for index in range(nearby):
        out_ref[owner_ref[0, index]] = near_ref[index * rows : (index + 1) * rows, :]
    for index in range(nearby, count):
        at = (index - nearby) * rows
        out_ref[owner_ref[0, index]] = product[at : at + rows]


def output_kernel(count, owner_ref, feature_ref, weight_ref, *refs):
    outs, held = refs[:-1], refs[-1]
    rows = feature_ref.shape[1]
    for index in range(count):
        held[index * rows : (index + 1) * rows, :] = feature_ref[owner_ref[0, index]]
    product = jnp.dot(held[...], weight_ref[...], preferred_element_type=jnp.float32)
    split_blocks(count, rows, product, outs)


def split_blocks(count, rows, product, outs):
    own, far_up, far_down, ups, downs = outs
    half_width = product.shape[1] // 2
    own[...] = product[:rows]
    for index in range(1, count - 1):
        side = ups if index % 2 else downs
        side[(index - 1) // 2] = product[index * rows : (index + 1) * rows]
    last = product[(count - 1) * rows :].astype(jnp.bfloat16)
    far_up[...] = last[:, :half_width]
    far_down[...] = last[:, half_width:]


def block_shapes(count, rows, width):
    own = jax.ShapeDtypeStruct((rows, width), jnp.float32)
    half = jax.ShapeDtypeStruct((rows, width // 2), jnp.bfloat16)
    side = jax.ShapeDtypeStruct((count // 2 - 1, rows, width), jnp.float32)
    return [own, half, half, side, side]


def residual_kernel(
    hidden_ref, own_ref, up_ref, down_ref, gain_ref, digit_ref, residual_ref, sent_ref
):
    width = hidden_ref.shape[1]
    summed = own_ref[...] + up_ref[...].astype(jnp.float32) + down_ref[...].astype(jnp.float32)
    residual = hidden_ref[...].astype(jnp.float32) + summed
    residual_ref[...] = residual
    sent_ref[:, :width] = norm_scale(residual, gain_ref[:1, :]).astype(jnp.bfloat16)
    sent_ref[:, width:] = digit_ref[...]


def expert_kernel(count, slots, slot_ref, held, *refs):
    subs = slot_ref.shape[1]
    gate_ups, downs, refs = refs[:subs], refs[subs : 2 * subs], refs[2 * subs :]
    outs, (units, total) = refs[:5], refs[5:]
    width = total.shape[1]
    inner = units.shape[1]
    rows = held.shape[0] // count
    digits = held[:, width:].astype(jnp.float32)
    lane = lax.broadcasted_iota(jnp.int32, digits.shape, 1)
    codes = digits * 32.0 + pltpu.roll(digits, HD // 2, 1)
    codes = jnp.where(lane < slots, codes, 0.0)
    whole = jnp.sum(codes, axis=1, keepdims=True)
    for shift in range(subs):
        mine = jnp.where(lane == slot_ref[0, shift], codes, 0.0)
        weight = jnp.sum(mine, axis=1, keepdims=True) / whole
        for start in range(0, inner, TILE):
            gate, up = [
                jnp.dot(
                    held[:, :width],
                    gate_ups[shift][:, column : column + TILE],
                    preferred_element_type=jnp.float32,
                )
                for column in (start, inner + start)
            ]
            units[:, start : start + TILE] = (jax.nn.silu(gate) * up).astype(jnp.bfloat16)
        for start in range(0, width, 2 * TILE):
            columns = slice(start, start + 2 * TILE)
            result = jnp.dot(
                units[...], downs[shift][:, columns], preferred_element_type=jnp.float32
            )
            result = result.astype(jnp.bfloat16).astype(jnp.float32) * weight
            if shift:
                result = result + total[:, columns]
            total[:, columns] = result
    split_blocks(count, rows, total, outs)


def attention_kernel(
    kv_count,
    length_ref,
    merged_ref,
    cos_ref,
    sin_ref,
    query_gain_ref,
    key_gain_ref,
    key_hbm,
    value_hbm,
    *refs,
):
    out_ref, queries, results, new_keys, new_values, key_ref, value_ref, start_ref, sems = refs[-9:]
    fetches = [
        pltpu.make_async_copy(key_hbm, key_ref, sems.at[0]),
        pltpu.make_async_copy(value_hbm, value_ref, sems.at[1]),
    ]
    fetches[0].start()
    rows = merged_ref.shape[1]
    heads = queries.shape[0] // rows
    group = heads // kv_count
    pool = key_ref.shape[0]
    per_block = merged_ref.shape[2] // HD
    scale = LOG2E / math.sqrt(HD)

    def head(index):
        block, slot = index // per_block, index % per_block
        return merged_ref[block, :, slot * HD : (slot + 1) * HD].astype(jnp.float32)

    def turned(values, gain):
        mean_square = jnp.mean(values * values, axis=-1, keepdims=True)
        values = values * lax.rsqrt(mean_square + EPSILON) * gain
        values = values * cos_ref[...] + pltpu.roll(values, HD // 2, 1) * sin_ref[...]
        return values.astype(jnp.bfloat16).astype(jnp.float32)

    total = jnp.int32(0)
    for row in range(rows):
        start_ref[row] = total
        total = total + length_ref[0, row]
    start_ref[rows] = total

    query_gain = query_gain_ref[...]
    key_gain = key_gain_ref[...]
    for kv in range(kv_count):
        columns = slice(kv * HD, (kv + 1) * HD)
        new_keys[:, columns] = turned(head(heads + kv), key_gain)
        new_values[:, columns] = head(heads + kv_count + kv)
    for index in range(heads):
        if index == heads // 2:
            fetches[1].start()
        queries[pl.ds(index, rows, stride=heads), :] = turned(head(index), query_gain)

    fetches[0].wait()

    place = lax.broadcasted_iota(jnp.int32, (WINDOW + ALIGN, heads), 0)
    kv_of_row = lax.broadcasted_iota(jnp.int32, (heads, HD), 0) // group

    def with_new(ref, window, fresh, row):
        new = jnp.broadcast_to(fresh[pl.ds(row, 1), :], (ALIGN, fresh.shape[1]))
        return jnp.concatenate([ref[window, :], new.astype(jnp.bfloat16)], axis=0)

    def window_of(row):
        first, last = start_ref[row], start_ref[row + 1]
        base = jnp.minimum(first // ALIGN * ALIGN, pool - WINDOW)
        return first - base, last - base, pl.ds(pl.multiple_of(base, ALIGN), WINDOW)

    def rows_of(row):
        return pl.ds(pl.multiple_of(row * heads, heads), heads)

    def scored(row):
        first, last, window = window_of(row)
        query = queries[rows_of(row), :]
        spread = jnp.concatenate(
            [jnp.where(kv_of_row == kv, query, 0.0) for kv in range(kv_count)], axis=1
        ).astype(jnp.bfloat16)
        scores = lax.dot_general(
            with_new(key_ref, window, new_keys, row),
            spread,
            (((1,), (1,)), ((), ())),
            preferred_element_type=jnp.float32,
        )
        inside = ((place >= first) & (place < last)) | (place == WINDOW)
        return jnp.where(inside, scores * scale, -1e30)

    def weighed(scores):
        raised = jnp.exp2(scores - jnp.max(scores, axis=0, keepdims=True))
        weights = raised * (1.0 / jnp.sum(raised, axis=0, keepdims=True))
        return weights.astype(jnp.bfloat16)

    def mix(row, weights):
        mixed = lax.dot_general(
            weights,
            with_new(value_ref, window_of(row)[2], new_values, row),
            (((0,), (0,)), ((), ())),
            preferred_element_type=jnp.float32,
        )
        results[rows_of(row), :] = jnp.concatenate(
            [
                mixed[kv * group : (kv + 1) * group, kv * HD : (kv + 1) * HD]
                for kv in range(kv_count)
            ],
            axis=0,
        )

    def body(step, carry):
        at = [step * UNROLL + inner for inner in range(UNROLL)]
        weights = [weighed(scores) for scores in [scored(row) for row in at]]

        @pl.when(step == 0)
        def _():
            fetches[1].wait()

        for row, weight in zip(at, weights):
            mix(row, weight)
        return carry

    lax.fori_loop(0, rows // UNROLL, body, 0)
    out_heads = out_ref.shape[2] // HD
    for index in range(heads):
        block, slot = index // out_heads, index % out_heads
        out_ref[block, :, slot * HD : (slot + 1) * HD] = results[
            pl.ds(index, rows, stride=heads), :
        ].astype(jnp.bfloat16)


def attend(merged, lengths, query_gain, key_gain, keys, values, count, swapped):
    rows = merged.shape[1]
    kv_count = keys.shape[1] // HD
    heads = merged.shape[0] * merged.shape[2] // HD - 2 * kv_count
    position = lengths.reshape(rows)
    frequency = ROPE_BASE ** (-jnp.arange(HD // 2, dtype=jnp.float32) * 2.0 / HD)
    angles = position.astype(jnp.float32)[:, None] * frequency[None, :]
    cosine, sine = jnp.cos(angles), jnp.sin(angles)
    return call(
        functools.partial(attention_kernel, kv_count),
        jax.ShapeDtypeStruct((count, rows, heads * HD // count), jnp.bfloat16),
        [SMEM] + [VMEM] * 5 + [HBM] * (2 + len(swapped)),
        (
            lengths,
            merged,
            jnp.concatenate([cosine, cosine], axis=1),
            jnp.concatenate([-sine, sine], axis=1),
            query_gain[None, :],
            key_gain[None, :],
            keys,
            values,
            *swapped,
        ),
        [
            pltpu.VMEM((heads * rows, HD), jnp.float32),
            pltpu.VMEM((heads * rows, HD), jnp.float32),
            pltpu.VMEM((rows, kv_count * HD), jnp.float32),
            pltpu.VMEM((rows, kv_count * HD), jnp.float32),
            pltpu.VMEM(keys.shape, keys.dtype),
            pltpu.VMEM(values.shape, values.dtype),
            pltpu.SMEM((rows + 1,), jnp.int32),
            pltpu.SemaphoreType.DMA((2,)),
        ],
        57,
        "ragged_attention",
    )


def on_device(
    hidden,
    lengths,
    key_cache,
    value_cache,
    expert_ids,
    gate_codes,
    expert_device,
    attention_gain,
    mixture_gain,
    query_gain,
    key_gain,
    project_weight,
    output_weight,
    expert_gate_up,
    expert_down,
):
    count, subs = lax.axis_size("dev"), lax.axis_size("sub")
    ring = Ring(count)
    rows, width = hidden.shape
    slots = expert_device.shape[0]

    def swapped(values):
        return [
            lax.ppermute(values, "sub", [(i, (i - shift) % subs) for i in range(subs)])
            for shift in range(1, subs)
        ]

    gate_ups = swapped(expert_gate_up[0])

    bf16 = jnp.bfloat16
    owners = ring.owners()
    dma = pltpu.SemaphoreType.DMA
    digits = call(
        digit_kernel,
        jax.ShapeDtypeStruct((rows, HD), bf16),
        [SMEM, VMEM, VMEM],
        (expert_device[None, :], expert_ids, gate_codes),
        [],
        4,
        "gate_digits",
    )
    columns = project_weight.shape[1]
    _, pieces = ring_gather(ring, hidden)
    (project_weight,) = loaded([project_weight], pieces[1], 50, "load_project")
    gain = tiled_gain(attention_gain)
    nearby = max(1, count - 3)
    near = call(
        functools.partial(project_near_kernel, rows),
        jax.ShapeDtypeStruct((nearby * rows, columns), bf16),
        [VMEM] * 3,
        (jnp.concatenate(pieces[:nearby], axis=0), gain, project_weight),
        [pltpu.VMEM((nearby * rows, width), bf16)],
        8,
        "project_near",
    )
    late = jnp.concatenate(pieces[nearby:], axis=0)
    blocks = call(
        functools.partial(project_kernel, count),
        jax.ShapeDtypeStruct((count, rows, columns), bf16),
        [SMEM] + [VMEM] * 4,
        (owners, near, late, gain, project_weight),
        [pltpu.VMEM(late.shape, bf16)],
        8,
        "project",
    )
    blocks = lax.all_to_all(blocks, "dev", split_axis=0, concat_axis=0, tiled=True)
    if columns % HD:
        blocks = jnp.transpose(blocks, (1, 0, 2)).reshape(1, rows, -1)
    attention = attend(
        blocks, lengths, query_gain, key_gain, key_cache[0], value_cache[0], count, [digits, *gate_ups]
    )
    down, attention = lax.optimization_barrier((expert_down[0], attention))
    downs = swapped(down)
    features = lax.all_to_all(attention, "dev", split_axis=0, concat_axis=0, tiled=True)
    (output_weight,) = loaded([output_weight], attention, 44, "load_output")
    own, *partial = call(
        functools.partial(output_kernel, count),
        block_shapes(count, rows, width),
        [SMEM, VMEM, VMEM],
        (owners, features, output_weight),
        [pltpu.VMEM((count * rows, output_weight.shape[0]), bf16)],
        8,
        "output_projection",
    )
    up, down, early = ring_scatter_sum(ring, *partial)
    own_gate_up = loaded([expert_gate_up[0]], early, 4, "load_gate_up")
    residual, sent = call(
        residual_kernel,
        [
            jax.ShapeDtypeStruct((rows, width), jnp.float32),
            jax.ShapeDtypeStruct((rows, width + HD), bf16),
        ],
        [VMEM] * 6,
        (hidden, own, up, down, tiled_gain(mixture_gain), digits),
        [],
        4,
        "residual_norm",
    )
    shifts = jnp.arange(subs, dtype=jnp.int32)[None, :]
    own_slots = lax.axis_index("dev") * subs + (lax.axis_index("sub") + shifts) % subs
    gathered, pieces = ring_gather(ring, sent)
    weights = list(own_gate_up)
    for index, gate_up in enumerate(gate_ups):
        weights += loaded([gate_up], pieces[2 * index + 1], 4, "load_gate_up")
    weights += loaded([expert_down[0]], pieces[2 * subs - 1], 4, "load_down")
    weights = [*weights, *downs]
    own, *partial = call(
        functools.partial(expert_kernel, count, slots),
        block_shapes(count, rows, width),
        [SMEM] + [VMEM] * (1 + 2 * subs),
        (own_slots, gathered, *weights),
        [
            pltpu.VMEM((count * rows, expert_down.shape[1]), bf16),
            pltpu.VMEM((count * rows, width), jnp.float32),
        ],
        18,
        "experts",
    )
    up, down, _ = ring_scatter_sum(ring, *partial)
    return (residual + own + up + down).astype(bf16)


def solution(mesh):
    return jax.shard_map(
        on_device,
        mesh=mesh,
        in_specs=(
            P(("groups", "dev", "sub"), None),
            P(("groups", "dev", "sub"), None),
            P(("groups", "dev", "sub"), None, None),
            P(("groups", "dev", "sub"), None, None),
            P(("groups", "dev", "sub"), None),
            P(("groups", "dev", "sub"), None),
            P(),
            P(),
            P(),
            P(),
            P(),
            P(None, "dev"),
            P("dev", None),
            P(("dev", "sub"), None, None),
            P(("dev", "sub"), None, None),
        ),
        out_specs=P(("groups", "dev", "sub"), None),
        check_vma=False,
    )
```

```python
import functools
import math

import jax
import jax.numpy as jnp
from jax import lax
from jax.experimental import pallas as pl
from jax.experimental.pallas import tpu as pltpu
from jax.sharding import PartitionSpec as P

HD = 128

EPSILON = 1e-06
ROPE_BASE = 1000000.0
LOG2E = 1.4426950408889634
LONGEST = 256
ALIGN = 16
WINDOW = LONGEST + ALIGN
UNROLL = 16
TILE = 256


def norm_scale(values, scale_gain):
    mean_square = jnp.mean(values * values, axis=-1, keepdims=True)
    return values * lax.rsqrt(mean_square + EPSILON) * scale_gain


def ring_order(count):
    return list(range(0, count, 2)) + list(range(1, count, 2))[::-1]


class Ring:
    def __init__(self, count):
        self.count = count
        self.far = count // 2
        order = ring_order(count)
        self.forward = [(order[i], order[(i + 1) % count]) for i in range(count)]
        self.backward = [(b, a) for a, b in self.forward]
        self.distances = [0]
        for step in range(1, self.far):
            self.distances += [step, -step]
        self.distances += [self.far]

    def ahead(self, values):
        return lax.ppermute(values, "dev", self.forward)

    def behind(self, values):
        return lax.ppermute(values, "dev", self.backward)

    def owners(self):
        count = self.count
        device = lax.axis_index("dev").astype(jnp.int32)
        index = lax.broadcasted_iota(jnp.int32, (1, count), 1)
        step = (index + 1) // 2
        distance = jnp.where(index % 2 == 1, step, -step)
        place = jnp.where(device % 2 == 0, device // 2, count - 1 - device // 2)
        place = place + distance
        place = jnp.where(place < 0, place + count, place)
        place = jnp.where(place >= count, place - count, place)
        return jnp.where(place < self.far, 2 * place, 2 * (count - 1 - place) + 1)


def ring_gather(ring, block):
    half_rows = block.shape[0] // 2
    up, down = block, block
    pieces = [block]
    for step in range(1, ring.far):
        up, down = ring.ahead(up), ring.behind(down)
        pieces += [down, up]
    pieces += [ring.ahead(up[:half_rows]), ring.behind(down[half_rows:])]
    return jnp.concatenate(pieces, axis=0), pieces


def ring_scatter_sum(ring, far_up, far_down, ups, downs):
    half_width = far_up.shape[1]
    sent = jnp.bfloat16
    up, down = ring.ahead(far_up), ring.behind(far_down)
    for distance in range(ring.far - 1, 0, -1):
        mine_up, mine_down = ups[distance - 1], downs[distance - 1]
        up, down = up.astype(jnp.float32), down.astype(jnp.float32)
        if distance == ring.far - 1:
            up = jnp.concatenate([mine_up[:, :half_width] + up, mine_up[:, half_width:]], axis=1)
            down = jnp.concatenate(
                [mine_down[:, :half_width], mine_down[:, half_width:] + down], axis=1
            )
        else:
            up, down = mine_up + up, mine_down + down
        up, down = ring.ahead(up.astype(sent)), ring.behind(down.astype(sent))
        if distance == 2:
            early = up
    return up, down, early


def whole_blocks(kinds):
    return [pl.BlockSpec(memory_space=kind) for kind in kinds]


def call(body, outs, ins, operands, scratch, limit, name, cost=100):
    return pl.pallas_call(
        body,
        out_shape=outs,
        in_specs=whole_blocks(ins),
        out_specs=jax.tree.map(lambda _: pl.BlockSpec(memory_space=pltpu.VMEM), outs),
        scratch_shapes=scratch,
        cost_estimate=pl.CostEstimate(
            flops=0, bytes_accessed=cost * 1024 * 1024, transcendentals=0
        ),
        compiler_params=pltpu.CompilerParams(vmem_limit_bytes=limit * 1024 * 1024),
        name=name,
    )(*operands)


VMEM, SMEM, HBM, ANY = pltpu.VMEM, pltpu.SMEM, pltpu.HBM, pl.ANY


def start_copies(pairs, sems):
    copies = [
        pltpu.make_async_copy(source, target, sems.at[index])
        for index, (source, target) in enumerate(pairs)
    ]
    for copy in copies:
        copy.start()
    return copies


def digit_kernel(holder_ref, ids_ref, codes_ref, out_ref):
    ids, codes = ids_ref[...], codes_ref[...]
    lane = lax.broadcasted_iota(jnp.int32, out_ref.shape, 1)
    high = jnp.zeros(out_ref.shape, jnp.float32)
    for expert in range(holder_ref.shape[1]):
        code = jnp.sum(jnp.where(ids == expert, codes, 0), axis=1, keepdims=True)
        slot = holder_ref[0, expert]
        high = high + jnp.where(lane == slot, (code >> 5).astype(jnp.float32), 0.0)
        high = high + jnp.where(lane == slot + HD // 2, (code & 31).astype(jnp.float32), 0.0)
    out_ref[...] = high.astype(jnp.bfloat16)


def tiled_gain(gain):
    return jnp.broadcast_to(gain[None, :], (8, gain.shape[0]))


def load_kernel(number, *refs):
    sources, targets, sems = refs[:number], refs[-1 - number : -1], refs[-1]
    for copy in start_copies(list(zip(sources, targets)), sems):
        copy.wait()


def loaded(arrays, after, limit, name):
    number = len(arrays)
    return call(
        functools.partial(load_kernel, number),
        [jax.ShapeDtypeStruct(array.shape, array.dtype) for array in arrays],
        [HBM] * number + [ANY],
        (*arrays, after),
        [pltpu.SemaphoreType.DMA((number,))],
        limit,
        name,
    )


def project(hidden_ref, gain_ref, weight_ref, held, rows):
    gain = gain_ref[:1, :]
    for start in range(0, hidden_ref.shape[0], rows):
        at = slice(start, start + rows)
        values = hidden_ref[at, :].astype(jnp.float32)
        held[at, :] = norm_scale(values, gain).astype(jnp.bfloat16)
    product = jnp.dot(held[...], weight_ref[...], preferred_element_type=jnp.float32)
    return product.astype(jnp.bfloat16)


def project_near_kernel(rows, hidden_ref, gain_ref, weight_ref, out_ref, held):
    out_ref[...] = project(hidden_ref, gain_ref, weight_ref, held, rows)


def project_kernel(count, owner_ref, near_ref, hidden_ref, gain_ref, weight_ref, *refs):
    out_ref, held = refs[-2:]
    rows = (near_ref.shape[0] + hidden_ref.shape[0]) // count
    nearby = near_ref.shape[0] // rows
    product = project(hidden_ref, gain_ref, weight_ref, held, rows)
    for index in range(nearby):
        out_ref[owner_ref[0, index]] = near_ref[index * rows : (index + 1) * rows, :]
    for index in range(nearby, count):
        at = (index - nearby) * rows
        out_ref[owner_ref[0, index]] = product[at : at + rows]


def output_kernel(count, owner_ref, feature_ref, weight_ref, *refs):
    outs, held = refs[:-1], refs[-1]
    rows = feature_ref.shape[1]
    for index in range(count):
        held[index * rows : (index + 1) * rows, :] = feature_ref[owner_ref[0, index]]
    product = jnp.dot(held[...], weight_ref[...], preferred_element_type=jnp.float32)
    split_blocks(count, rows, product, outs)


def split_blocks(count, rows, product, outs):
    own, far_up, far_down, ups, downs = outs
    half_width = product.shape[1] // 2
    own[...] = product[:rows]
    for index in range(1, count - 1):
        side = ups if index % 2 else downs
        side[(index - 1) // 2] = product[index * rows : (index + 1) * rows]
    last = product[(count - 1) * rows :].astype(jnp.bfloat16)
    far_up[...] = last[:, :half_width]
    far_down[...] = last[:, half_width:]


def block_shapes(count, rows, width):
    own = jax.ShapeDtypeStruct((rows, width), jnp.float32)
    half = jax.ShapeDtypeStruct((rows, width // 2), jnp.bfloat16)
    side = jax.ShapeDtypeStruct((count // 2 - 1, rows, width), jnp.float32)
    return [own, half, half, side, side]


def residual_kernel(
    hidden_ref, own_ref, up_ref, down_ref, gain_ref, digit_ref, residual_ref, sent_ref
):
    width = hidden_ref.shape[1]
    summed = own_ref[...] + up_ref[...].astype(jnp.float32) + down_ref[...].astype(jnp.float32)
    residual = hidden_ref[...].astype(jnp.float32) + summed
    residual_ref[...] = residual
    sent_ref[:, :width] = norm_scale(residual, gain_ref[:1, :]).astype(jnp.bfloat16)
    sent_ref[:, width:] = digit_ref[...]


def expert_kernel(count, slots, slot_ref, held, *refs):
    subs = slot_ref.shape[1]
    gate_ups, downs, refs = refs[:subs], refs[subs : 2 * subs], refs[2 * subs :]
    outs, (units, total) = refs[:5], refs[5:]
    width = total.shape[1]
    inner = units.shape[1]
    rows = held.shape[0] // count
    digits = held[:, width:].astype(jnp.float32)
    lane = lax.broadcasted_iota(jnp.int32, digits.shape, 1)
    codes = digits * 32.0 + pltpu.roll(digits, HD // 2, 1)
    codes = jnp.where(lane < slots, codes, 0.0)
    whole = jnp.sum(codes, axis=1, keepdims=True)
    for shift in range(subs):
        mine = jnp.where(lane == slot_ref[0, shift], codes, 0.0)
        weight = jnp.sum(mine, axis=1, keepdims=True) / whole
        for start in range(0, inner, TILE):
            gate, up = [
                jnp.dot(
                    held[:, :width],
                    gate_ups[shift][:, column : column + TILE],
                    preferred_element_type=jnp.float32,
                )
                for column in (start, inner + start)
            ]
            units[:, start : start + TILE] = (jax.nn.silu(gate) * up).astype(jnp.bfloat16)
        for start in range(0, width, 4 * TILE):
            columns = slice(start, start + 4 * TILE)
            result = jnp.dot(
                units[...], downs[shift][:, columns], preferred_element_type=jnp.float32
            )
            result = result.astype(jnp.bfloat16).astype(jnp.float32) * weight
            if shift:
                result = result + total[:, columns]
            total[:, columns] = result
    split_blocks(count, rows, total, outs)


def attention_kernel(
    kv_count,
    length_ref,
    merged_ref,
    cos_ref,
    sin_ref,
    query_gain_ref,
    key_gain_ref,
    key_hbm,
    value_hbm,
    *refs,
):
    out_ref, queries, results, new_keys, new_values, key_ref, value_ref, start_ref, sems = refs[-9:]
    fetches = [
        pltpu.make_async_copy(key_hbm, key_ref, sems.at[0]),
        pltpu.make_async_copy(value_hbm, value_ref, sems.at[1]),
    ]
    fetches[0].start()
    rows = merged_ref.shape[1]
    heads = queries.shape[0] // rows
    group = heads // kv_count
    pool = key_ref.shape[0]
    per_block = merged_ref.shape[2] // HD
    scale = LOG2E / math.sqrt(HD)

    def head(index):
        block, slot = index // per_block, index % per_block
        return merged_ref[block, :, slot * HD : (slot + 1) * HD].astype(jnp.float32)

    def turned(values, gain):
        mean_square = jnp.mean(values * values, axis=-1, keepdims=True)
        values = values * lax.rsqrt(mean_square + EPSILON) * gain
        values = values * cos_ref[...] + pltpu.roll(values, HD // 2, 1) * sin_ref[...]
        return values.astype(jnp.bfloat16).astype(jnp.float32)

    total = jnp.int32(0)
    for row in range(rows):
        start_ref[row] = total
        total = total + length_ref[0, row]
    start_ref[rows] = total

    query_gain = query_gain_ref[...]
    key_gain = key_gain_ref[...]
    for kv in range(kv_count):
        columns = slice(kv * HD, (kv + 1) * HD)
        new_keys[:, columns] = turned(head(heads + kv), key_gain)
        new_values[:, columns] = head(heads + kv_count + kv)
    for index in range(heads):
        if index == heads // 2:
            fetches[1].start()
        queries[pl.ds(index, rows, stride=heads), :] = turned(head(index), query_gain)

    fetches[0].wait()

    place = lax.broadcasted_iota(jnp.int32, (WINDOW + ALIGN, heads), 0)
    kv_of_row = lax.broadcasted_iota(jnp.int32, (heads, HD), 0) // group

    def with_new(ref, window, fresh, row):
        new = jnp.broadcast_to(fresh[pl.ds(row, 1), :], (ALIGN, fresh.shape[1]))
        return jnp.concatenate([ref[window, :], new.astype(jnp.bfloat16)], axis=0)

    def window_of(row):
        first, last = start_ref[row], start_ref[row + 1]
        base = jnp.minimum(first // ALIGN * ALIGN, pool - WINDOW)
        return first - base, last - base, pl.ds(pl.multiple_of(base, ALIGN), WINDOW)

    def rows_of(row):
        return pl.ds(pl.multiple_of(row * heads, heads), heads)

    def scored(row):
        first, last, window = window_of(row)
        query = queries[rows_of(row), :]
        spread = jnp.concatenate(
            [jnp.where(kv_of_row == kv, query, 0.0) for kv in range(kv_count)], axis=1
        ).astype(jnp.bfloat16)
        scores = lax.dot_general(
            with_new(key_ref, window, new_keys, row),
            spread,
            (((1,), (1,)), ((), ())),
            preferred_element_type=jnp.float32,
        )
        inside = ((place >= first) & (place < last)) | (place == WINDOW)
        return jnp.where(inside, scores * scale, -1e30)

    def weighed(scores):
        raised = jnp.exp2(scores - jnp.max(scores, axis=0, keepdims=True))
        weights = raised * (1.0 / jnp.sum(raised, axis=0, keepdims=True))
        return weights.astype(jnp.bfloat16)

    def mix(row, weights):
        mixed = lax.dot_general(
            weights,
            with_new(value_ref, window_of(row)[2], new_values, row),
            (((0,), (0,)), ((), ())),
            preferred_element_type=jnp.float32,
        )
        results[rows_of(row), :] = jnp.concatenate(
            [
                mixed[kv * group : (kv + 1) * group, kv * HD : (kv + 1) * HD]
                for kv in range(kv_count)
            ],
            axis=0,
        )

    def body(step, carry):
        at = [step * UNROLL + inner for inner in range(UNROLL)]
        weights = [weighed(scores) for scores in [scored(row) for row in at]]

        @pl.when(step == 0)
        def _():
            fetches[1].wait()

        for row, weight in zip(at, weights):
            mix(row, weight)
        return carry

    lax.fori_loop(0, rows // UNROLL, body, 0)
    out_heads = out_ref.shape[2] // HD
    for index in range(heads):
        block, slot = index // out_heads, index % out_heads
        out_ref[block, :, slot * HD : (slot + 1) * HD] = results[
            pl.ds(index, rows, stride=heads), :
        ].astype(jnp.bfloat16)


def attend(merged, lengths, query_gain, key_gain, keys, values, count, swapped):
    rows = merged.shape[1]
    kv_count = keys.shape[1] // HD
    heads = merged.shape[0] * merged.shape[2] // HD - 2 * kv_count
    position = lengths.reshape(rows)
    frequency = ROPE_BASE ** (-jnp.arange(HD // 2, dtype=jnp.float32) * 2.0 / HD)
    angles = position.astype(jnp.float32)[:, None] * frequency[None, :]
    cosine, sine = jnp.cos(angles), jnp.sin(angles)
    return call(
        functools.partial(attention_kernel, kv_count),
        jax.ShapeDtypeStruct((count, rows, heads * HD // count), jnp.bfloat16),
        [SMEM] + [VMEM] * 5 + [HBM] * (2 + len(swapped)),
        (
            lengths,
            merged,
            jnp.concatenate([cosine, cosine], axis=1),
            jnp.concatenate([-sine, sine], axis=1),
            query_gain[None, :],
            key_gain[None, :],
            keys,
            values,
            *swapped,
        ),
        [
            pltpu.VMEM((heads * rows, HD), jnp.float32),
            pltpu.VMEM((heads * rows, HD), jnp.float32),
            pltpu.VMEM((rows, kv_count * HD), jnp.float32),
            pltpu.VMEM((rows, kv_count * HD), jnp.float32),
            pltpu.VMEM(keys.shape, keys.dtype),
            pltpu.VMEM(values.shape, values.dtype),
            pltpu.SMEM((rows + 1,), jnp.int32),
            pltpu.SemaphoreType.DMA((2,)),
        ],
        57,
        "ragged_attention",
    )


def on_device(
    hidden,
    lengths,
    key_cache,
    value_cache,
    expert_ids,
    gate_codes,
    expert_device,
    attention_gain,
    mixture_gain,
    query_gain,
    key_gain,
    project_weight,
    output_weight,
    expert_gate_up,
    expert_down,
):
    count, subs = lax.axis_size("dev"), lax.axis_size("sub")
    ring = Ring(count)
    rows, width = hidden.shape
    slots = expert_device.shape[0]

    def swapped(values):
        return [
            lax.ppermute(values, "sub", [(i, (i - shift) % subs) for i in range(subs)])
            for shift in range(1, subs)
        ]

    gate_ups = swapped(expert_gate_up[0])

    bf16 = jnp.bfloat16
    owners = ring.owners()
    dma = pltpu.SemaphoreType.DMA
    digits = call(
        digit_kernel,
        jax.ShapeDtypeStruct((rows, HD), bf16),
        [SMEM, VMEM, VMEM],
        (expert_device[None, :], expert_ids, gate_codes),
        [],
        4,
        "gate_digits",
    )
    columns = project_weight.shape[1]
    _, pieces = ring_gather(ring, hidden)
    (project_weight,) = loaded([project_weight], pieces[1], 50, "load_project")
    gain = tiled_gain(attention_gain)
    nearby = max(1, count - 3)
    near = call(
        functools.partial(project_near_kernel, rows),
        jax.ShapeDtypeStruct((nearby * rows, columns), bf16),
        [VMEM] * 3,
        (jnp.concatenate(pieces[:nearby], axis=0), gain, project_weight),
        [pltpu.VMEM((nearby * rows, width), bf16)],
        8,
        "project_near",
    )
    late = jnp.concatenate(pieces[nearby:], axis=0)
    blocks = call(
        functools.partial(project_kernel, count),
        jax.ShapeDtypeStruct((count, rows, columns), bf16),
        [SMEM] + [VMEM] * 4,
        (owners, near, late, gain, project_weight),
        [pltpu.VMEM(late.shape, bf16)],
        8,
        "project",
    )
    blocks = lax.all_to_all(blocks, "dev", split_axis=0, concat_axis=0, tiled=True)
    if columns % HD:
        blocks = jnp.transpose(blocks, (1, 0, 2)).reshape(1, rows, -1)
    attention = attend(
        blocks, lengths, query_gain, key_gain, key_cache[0], value_cache[0], count, [digits, *gate_ups]
    )
    down, attention = lax.optimization_barrier((expert_down[0], attention))
    downs = swapped(down)
    features = lax.all_to_all(attention, "dev", split_axis=0, concat_axis=0, tiled=True)
    (output_weight,) = loaded([output_weight], attention, 44, "load_output")
    own, *partial = call(
        functools.partial(output_kernel, count),
        block_shapes(count, rows, width),
        [SMEM, VMEM, VMEM],
        (owners, features, output_weight),
        [pltpu.VMEM((count * rows, output_weight.shape[0]), bf16)],
        8,
        "output_projection",
    )
    up, down, early = ring_scatter_sum(ring, *partial)
    own_gate_up = loaded([expert_gate_up[0]], early, 4, "load_gate_up")
    residual, sent = call(
        residual_kernel,
        [
            jax.ShapeDtypeStruct((rows, width), jnp.float32),
            jax.ShapeDtypeStruct((rows, width + HD), bf16),
        ],
        [VMEM] * 6,
        (hidden, own, up, down, tiled_gain(mixture_gain), digits),
        [],
        4,
        "residual_norm",
    )
    shifts = jnp.arange(subs, dtype=jnp.int32)[None, :]
    own_slots = lax.axis_index("dev") * subs + (lax.axis_index("sub") + shifts) % subs
    gathered, pieces = ring_gather(ring, sent)
    weights = list(own_gate_up)
    for index, gate_up in enumerate(gate_ups):
        weights += loaded([gate_up], pieces[2 * index + 1], 4, "load_gate_up")
    weights += loaded([expert_down[0]], pieces[2 * subs - 1], 4, "load_down")
    weights = [*weights, *downs]
    own, *partial = call(
        functools.partial(expert_kernel, count, slots),
        block_shapes(count, rows, width),
        [SMEM] + [VMEM] * (1 + 2 * subs),
        (own_slots, gathered, *weights),
        [
            pltpu.VMEM((count * rows, expert_down.shape[1]), bf16),
            pltpu.VMEM((count * rows, width), jnp.float32),
        ],
        18,
        "experts",
    )
    up, down, _ = ring_scatter_sum(ring, *partial)
    return (residual + own + up + down).astype(bf16)


def solution(mesh):
    return jax.shard_map(
        on_device,
        mesh=mesh,
        in_specs=(
            P(("groups", "dev", "sub"), None),
            P(("groups", "dev", "sub"), None),
            P(("groups", "dev", "sub"), None, None),
            P(("groups", "dev", "sub"), None, None),
            P(("groups", "dev", "sub"), None),
            P(("groups", "dev", "sub"), None),
            P(),
            P(),
            P(),
            P(),
            P(),
            P(None, "dev"),
            P("dev", None),
            P(("dev", "sub"), None, None),
            P(("dev", "sub"), None, None),
        ),
        out_specs=P(("groups", "dev", "sub"), None),
        check_vma=False,
    )
```
